512 devices in a mesh: win: 32 (over y, z_lo, core), grp: 16 (over x, z_hi).
Axes of the slice: x: 4, y: 8, z: 8 (z_hi: 4, z_lo: 2; z = z_hi * 2 + z_lo), core: 2. Of those that a mesh axis runs over, the one named last changes fastest.
Arguments:
- spectra: bfloat16 [32, 4096, 2, 2048], P(None, 'win', None, 'grp'), may hold values from -6 to 6
- freq_bins: int32 [32], replicated, may hold values from 8 to 39
- slowness: float32 [4], replicated, may hold values from 0.04 to 0.12
- positions: int32 [2048], replicated, may hold values from 0 to 2047, each once
Outputs:
- image: float32 [32, 4, 2048], P('win', None, 'grp')
The draws below stay inside these ranges and needn't reach their ends.
Inputs may be any that keep to these rules, and one draw needn't show every extreme that they name: `positions`: every grid cell holds exactly one receiver.
All inputs are finite; a program needn't handle non-finite values.
Results may differ from the reference program's by a relative error of at most 0.0003.
Values may be sent and summed in bfloat16 or wider, within the bound.
A program may use at most 64 MiB of HBM per device.

```python
import math
import jax
import jax.numpy as jnp
from jax import lax

RECEIVERS = 2048
GX = 32
WINDOWS = 4096
FREQS = 32
SOURCES = 64
DEPTHS = 4


def place_ends(result, rng, low, top_value):
    longest = result.shape.index(max(result.shape))
    spots = []
    for shift in (0, 1):
        where = [jax.random.randint(jax.random.fold_in(rng, axis), (), 0, length) for axis, length in enumerate(result.shape)]
        where[longest] = (where[longest] + shift) % result.shape[longest]
        spots.append(tuple(where))
    return result.at[spots[0]].set(low).at[spots[1]].set(top_value)


def with_spikes(array, key, source, target, shards_of, factor):
    owner, partner = [(jnp.arange(array.shape[dim]) // (array.shape[dim] // shards_of)).reshape([-1 if axis == dim else 1 for axis in range(array.ndim)]) for dim in (source, target)]
    chosen = jax.random.permutation(key, shards_of)[partner]
    strong = (owner == chosen) | (owner == (partner + shards_of // 2) % shards_of)
    return jnp.where(strong, factor * array, array)


def shard_levels(key, extent, split, least, top_value):
    level, own = 1.0, jax.random.fold_in(key, 6)
    for dim, blocks in split:
        steps = jnp.exp(jax.random.uniform(jax.random.fold_in(own, dim), (blocks,), jnp.float32, least / len(split), top_value / len(split)))
        level = level * jnp.repeat(steps, extent[dim] // blocks).reshape([-1 if axis == dim else 1 for axis in range(len(extent))])
    return level


def gaussian_with(key, dims, width, most, cuts, heavy, held_as=jnp.bfloat16):
    drawn = width * jax.random.normal(key, dims, jnp.float32)
    if cuts:
        drawn = drawn * shard_levels(key, dims, cuts, -0.22, 0.18)
    return jnp.clip(with_spikes(drawn, jax.random.fold_in(key, 3), *heavy), -most, most).astype(held_as)


def setup_inputs(seed: int = 0) -> dict:
    seeds = jax.random.split(jax.random.key(seed), 5)
    return {
        "spectra": gaussian_with(seeds[0], (FREQS, WINDOWS, 2, RECEIVERS), 1.0, 6.0, ((1, 32), (3, 16)), (1, 0, 32, 2.75)),
        "freq_bins": place_ends(jax.random.randint(seeds[1], (FREQS,), 8, 40), jax.random.fold_in(seeds[1], 1), 8, 39).astype(jnp.int32),
        "slowness": jnp.clip(jnp.exp(jax.random.uniform(seeds[2], (DEPTHS,), jnp.float32, math.log(0.04), math.log(0.12))), 0.04, 0.12),
        "positions": jax.random.permutation(seeds[3], RECEIVERS).astype(jnp.int32),
    }


HIGHEST_PRECISION = lax.Precision.HIGHEST

def dft_tables(length):
    indices = jnp.arange(length, dtype=jnp.int32)
    products = indices[:, None] * indices[None, :] % length
    phases = products.astype(jnp.float32) * (2.0 * math.pi / length)
    return (jnp.cos(phases), jnp.sin(phases))

def wave_squares(grid_x, grid_y):
    x_index = jnp.arange(grid_x, dtype=jnp.int32)
    y_index = jnp.arange(grid_y, dtype=jnp.int32)
    x_signed = jnp.where(x_index < (grid_x + 1) // 2, x_index, x_index - grid_x).astype(jnp.float32) * (2.0 * math.pi / grid_x)
    y_signed = jnp.where(y_index < (grid_y + 1) // 2, y_index, y_index - grid_y).astype(jnp.float32) * (2.0 * math.pi / grid_y)
    return x_signed[:, None] ** 2 + y_signed[None, :] ** 2

def along_y(field, table):
    return jnp.einsum('kxy,yv->kxv', field, table, precision=HIGHEST_PRECISION)

def along_x(table, field):
    return jnp.einsum('ux,kxv->kuv', table, field, precision=HIGHEST_PRECISION)

def migrate(field_re, field_im, wavenumber, positions, grid_x):
    shot_count, cell_count = field_re.shape
    grid_y = cell_count // grid_x
    grid_re = jnp.zeros_like(field_re).at[:, positions].set(field_re).reshape(shot_count, grid_x, grid_y)
    grid_im = jnp.zeros_like(field_im).at[:, positions].set(field_im).reshape(shot_count, grid_x, grid_y)
    cos_x, sin_x = dft_tables(grid_x)
    cos_y, sin_y = dft_tables(grid_y)
    section_re = along_y(grid_re, cos_y) + along_y(grid_im, sin_y)
    section_im = along_y(grid_im, cos_y) - along_y(grid_re, sin_y)
    spec_re = along_x(cos_x, section_re) + along_x(sin_x, section_im)
    spec_im = along_x(cos_x, section_im) - along_x(sin_x, section_re)
    squares = wave_squares(grid_x, grid_y)
    factor = 1.0 / math.sqrt(grid_x * grid_y)
    energies = []
    for depth_step in range(wavenumber.shape[0]):
        excess = wavenumber[depth_step] ** 2 - squares
        vertical = jnp.sqrt(jnp.maximum(excess, 0.0))
        damping = jnp.exp(-jnp.sqrt(jnp.maximum(-excess, 0.0)))
        shift_re = damping * jnp.cos(vertical)
        shift_im = damping * jnp.sin(vertical)
        spec_re, spec_im = (spec_re * shift_re - spec_im * shift_im, spec_re * shift_im + spec_im * shift_re)
        back_re = along_y(spec_re, cos_y) - along_y(spec_im, sin_y)
        back_im = along_y(spec_im, cos_y) + along_y(spec_re, sin_y)
        picture = (along_x(cos_x, back_re) - along_x(sin_x, back_im)) * factor
        energies.append((picture * picture).reshape(shot_count, cell_count))
    return jnp.stack(energies, axis=1)

def inner_windows(first_part, second_part):
    return jnp.dot(first_part.T, second_part, precision=HIGHEST_PRECISION)

def reference(spectra, freq_bins, slowness, positions):
    stride = RECEIVERS // SOURCES
    wavenumbers = freq_bins.astype(jnp.float32)[:, None] * slowness[None, :]

    def one_freq(carried, inputs):
        freq_block, wavenumber = inputs
        traces = freq_block.astype(jnp.float32)
        source_data = traces[:, :, ::stride]
        gram_re = (inner_windows(source_data[:, 0], traces[:, 0]) + inner_windows(source_data[:, 1], traces[:, 1])) / WINDOWS
        gram_im = (inner_windows(source_data[:, 0], traces[:, 1]) - inner_windows(source_data[:, 1], traces[:, 0])) / WINDOWS
        energies = migrate(gram_re, gram_im, wavenumber, positions, GX)
        return (carried, lax.optimization_barrier(jnp.sum(energies, axis=0)) / SOURCES)
    _, stacked = lax.scan(one_freq, jnp.zeros((), jnp.float32), (spectra, wavenumbers))
    return stacked
```

```python
import functools
import math

import jax
import jax.numpy as jnp
import numpy as np
from jax import lax
from jax.experimental import pallas as pl
from jax.experimental.pallas import tpu as pltpu
from jax.sharding import PartitionSpec as P

MESH = pl.DeviceIdType.MESH
GY = 64
LANES = 128
SHOTS = 4
F32, BF16 = jnp.float32, jnp.bfloat16


def split(table):
    high = table.astype(BF16)
    return high, (table - high.astype(F32)).astype(BF16)


def dot(a, b):
    return jnp.dot(a, b, preferred_element_type=F32)


def dot_lanes(a, b):
    return lax.dot_general(a, b, (((1,), (1,)), ((), ())), preferred_element_type=F32)


def dot3(a, b_high, b_low):
    high, low = split(a)
    width = b_high.shape[1]
    both = dot(high, jnp.concatenate([b_high, b_low], axis=1))
    return both[:, :width] + both[:, width:] + dot(low, b_high)


def np_split(table):
    table = table.astype(np.float32)
    high = table.astype(BF16)
    return high, (table - high.astype(np.float32)).astype(BF16)


def tables(grid_x):
    def angles(length):
        index = np.arange(length)
        return (index[:, None] * index[None, :] % length) * (2.0 * math.pi / length)

    cos_x, sin_x = np.cos(angles(grid_x)), np.sin(angles(grid_x))
    cos_y, sin_y = np.cos(angles(GY)), np.sin(angles(GY))
    shots = np.eye(SHOTS)
    block_cos, block_sin = np.kron(shots, cos_x), np.kron(shots, sin_x)
    rows_y = np.concatenate([cos_y, sin_y], axis=0)
    forward_x = np.concatenate([block_cos, block_sin], axis=1)
    inverse_x = np.concatenate([block_cos, -block_sin], axis=1)
    to_re = np.concatenate([cos_y, -sin_y], axis=0)
    to_im = np.concatenate([sin_y, cos_y], axis=0)
    none = np.zeros_like(to_re)
    inverse_y = np.block([[to_re, none, to_im, none], [none, to_re, none, to_im]])
    x_index, y_index = np.arange(grid_x), np.arange(GY)
    x_signed = np.where(x_index < (grid_x + 1) // 2, x_index, x_index - grid_x).astype(np.float32) * np.float32(
        2.0 * math.pi / grid_x
    )
    y_signed = np.where(y_index < (GY + 1) // 2, y_index, y_index - GY).astype(np.float32) * np.float32(
        2.0 * math.pi / GY
    )
    squares = x_signed[:, None] ** 2 + y_signed[None, :] ** 2
    return (
        np.stack(np_split(rows_y)),
        np.stack(np_split(forward_x)),
        np.stack(np_split(inverse_x)),
        np.stack(np_split(inverse_y)),
        np.concatenate([squares, squares], axis=1).astype(np.float32),
    )


def iota(shape, dim):
    return lax.broadcasted_iota(jnp.int32, shape, dim)


def one_hot(condition):
    return jnp.where(condition, 1.0, 0.0).astype(BF16)


def kernel(
    n_grp, n_win, side, windows,
    spectra, positions, freq_bins, slowness, rows_y, forward_x, inverse_x, inverse_y, squares,
    out,
    u, turned, picked, perm_picked, gram, got_gram, tiles, got_tiles, energy, got_energy,
    y_phase, x_mask, shift,
    local_sem, core_sem, ag_send, ag_recv, rs_send, rs_recv, aa_send, aa_recv, en_send, en_recv,
):
    n_freq = n_win // 2
    grid_x = 2 * n_grp
    rows = 2 * windows
    win, grp = lax.axis_index("win"), lax.axis_index("grp")
    core, chip = lax.rem(win, 2), lax.div(win, 2)
    zh, x = lax.rem(grp, side), lax.div(grp, side)
    other = 1 - core

    def peer_chip(d):
        return lax.rem(chip + d, n_freq)

    def device(chip_at, core_at, grp_at):
        return (chip_at * 2 + core_at, grp_at)

    own_copy = pltpu.make_async_copy(spectra.at[:, core], u.at[:, core], local_sem.at[0])
    own_copy.start()

    barrier = pltpu.get_barrier_semaphore()
    pl.semaphore_signal(barrier, inc=1, device_id=device(chip, other, grp), device_id_type=MESH)
    for d in range(1, n_grp):
        pl.semaphore_signal(barrier, inc=1, device_id=device(chip, core, lax.rem(grp + d, n_grp)), device_id_type=MESH)
    for d in range(1, n_freq):
        pl.semaphore_signal(barrier, inc=1, device_id=device(peer_chip(d), core, grp), device_id_type=MESH)
    pl.semaphore_wait(barrier, n_grp + n_freq - 1)

    core_copy = pltpu.make_async_remote_copy(
        src_ref=spectra.at[:, other], dst_ref=u.at[:, core], send_sem=core_sem.at[0], recv_sem=core_sem.at[1],
        device_id=device(chip, other, grp), device_id_type=MESH,
    )
    core_copy.start()
    own_copy.wait()
    core_copy.wait()

    mine = jnp.zeros((n_freq * SHOTS, 2 * rows), F32)
    row, lane = iota((n_freq * SHOTS, LANES), 0), iota((n_freq * SHOTS, LANES), 1)
    for q in range(n_freq):
        pick = one_hot(lane == (row - SHOTS * q) * (LANES // SHOTS))
        mine += dot_lanes(pick, u[q].reshape(2 * rows, LANES))
    picked[grp] = mine.astype(BF16)

    def source_copy(holder, target, slot):
        return pltpu.make_async_remote_copy(
            src_ref=picked.at[holder], dst_ref=picked.at[holder], send_sem=ag_send.at[slot], recv_sem=ag_recv.at[slot],
            device_id=device(chip, core, target), device_id_type=MESH,
        )

    sends = []
    for d in range(1, side):
        sends.append(source_copy(grp, x * side + lax.rem(zh + d, side), d))
        sends[-1].start()
    for e in range(1, side):
        sends.append(source_copy(grp, lax.rem(x + e, side) * side + zh, e * side))
        sends[-1].start()

    row, lane = iota((rows, rows), 0), iota((rows, rows), 1)
    even = lax.rem(row, 2) == 0
    swap = jnp.where(even & (lane == row + 1), 1.0, jnp.where(~even & (lane == row - 1), -1.0, 0.0)).astype(BF16)

    def turn(i, carry):
        for half in range(2):
            turned[i, half] = dot(swap, u[i, half]).astype(BF16)
        return carry

    lax.fori_loop(0, n_freq, turn, 0)

    where = positions[...]
    cell_x, cell_y = lax.shift_right_logical(where, 6), jnp.bitwise_and(where, GY - 1)
    receivers = n_grp * LANES
    y_hot = one_hot(iota((GY, receivers), 0) == cell_y)
    y_phase[0:LANES] = dot(rows_y[0], y_hot).astype(BF16)
    y_phase[LANES:] = dot(rows_y[1], y_hot).astype(BF16)
    x_mask[...] = one_hot(iota((grid_x, receivers), 0) == cell_x)
    freq = freq_bins[win].astype(F32)
    sign = jnp.where(iota((grid_x, LANES), 1) < GY, -1.0, 1.0)
    total_re, total_im = None, None
    for k in range(4):
        kappa = freq * slowness[k]
        excess = kappa * kappa - squares[...]
        vertical = jnp.sqrt(jnp.maximum(excess, 0.0))
        damping = jnp.exp(-jnp.sqrt(jnp.maximum(-excess, 0.0)))
        step_re, step_im = damping * jnp.cos(vertical), damping * jnp.sin(vertical)
        if k == 0:
            total_re, total_im = step_re, step_im
        else:
            total_re, total_im = total_re * step_re - total_im * step_im, total_re * step_im + total_im * step_re
        shift[k, 0] = total_re
        shift[k, 1] = sign * total_im

    for d in range(1, side):
        origin = x * side + lax.rem(zh + side - d, side)
        source_copy(origin, grp, d).wait_recv()
        for e in range(1, side):
            sends.append(source_copy(origin, lax.rem(x + e, side) * side + zh, e * side + d))
            sends[-1].start()
    for e in range(1, side):
        for d in range(side):
            origin = lax.rem(x + side - e, side) * side + lax.rem(zh + side - d, side)
            source_copy(origin, grp, e * side + d).wait_recv()

    group = 16 // SHOTS
    height = 16 * n_grp
    row, lane = iota((height, height), 0), iota((height, height), 1)
    n_src = SHOTS * n_grp
    q_of, src_of = lax.div(row, n_src), lax.rem(row, n_src)
    reorder = one_hot(lane == lax.div(src_of, SHOTS) * 16 + q_of * SHOTS + lax.rem(src_of, SHOTS))
    for a in range(n_freq * SHOTS // 16):
        block = picked[:, 16 * a : 16 * (a + 1), :].reshape(height, 2 * rows)
        perm_picked[group * a : group * (a + 1)] = dot(reorder, block).astype(BF16).reshape(group, n_src, 2 * rows)

    def gram_copy(d):
        return pltpu.make_async_remote_copy(
            src_ref=gram.at[peer_chip(d)], dst_ref=got_gram.at[d], send_sem=rs_send.at[d], recv_sem=rs_recv.at[d],
            device_id=device(peer_chip(d), core, grp), device_id_type=MESH,
        )

    for d in list(range(1, n_freq)) + [0]:
        q = peer_chip(d)
        right = jnp.concatenate([u[q].reshape(2 * rows, LANES), turned[q].reshape(2 * rows, LANES)], axis=1)
        gram[q] = dot(perm_picked[q], right)
        if d:
            sends.append(gram_copy(d))
            sends[-1].start()
    total = gram[chip]
    for d in range(1, n_freq):
        gram_copy(d).wait_recv()
        total += got_gram[d]

    real, imag = total[:, :LANES], total[:, LANES:]
    upper = lax.rem(iota((n_src, LANES), 0), 8) < SHOTS
    first = jnp.where(upper, real, pltpu.roll(imag, SHOTS, 0))
    second = jnp.where(upper, pltpu.roll(real, n_src - SHOTS, 0), imag)
    for a in range(n_grp // 2):
        tiles[2 * a] = first[8 * a : 8 * a + 8]
        tiles[2 * a + 1] = second[8 * a : 8 * a + 8]

    def tile_copy(d):
        target = lax.rem(grp + d, n_grp)
        return pltpu.make_async_remote_copy(
            src_ref=tiles.at[target], dst_ref=got_tiles.at[grp], send_sem=aa_send.at[d], recv_sem=aa_recv.at[d],
            device_id=device(chip, core, target), device_id_type=MESH,
        )

    for d in range(1, n_grp):
        sends.append(tile_copy(d))
        sends[-1].start()
    got_tiles[grp] = tiles[grp]
    for d in range(1, n_grp):
        tile_copy(d).wait_recv()

    field = jnp.concatenate([got_tiles[g] for g in range(n_grp)], axis=1)
    field_high = field.astype(BF16).astype(F32)
    field_low = field - field_high
    mask = x_mask[...]

    def placed(part):
        return jnp.concatenate(
            [jnp.broadcast_to(part[i : i + 1], (grid_x, receivers)).astype(BF16) * mask for i in range(2 * SHOTS)], axis=0
        )

    section = dot_lanes(placed(field_high), y_phase[...])
    section = section[:, :LANES] + section[:, LANES:] + dot_lanes(placed(field_low), y_phase[0:LANES])
    half = SHOTS * grid_x
    lower = iota((half, LANES), 1) < GY
    plus_minus = jnp.where(lower, 1.0, -1.0)
    section = plus_minus * section[:half] + pltpu.roll(section[half:], GY, 1)
    turned_section = plus_minus * pltpu.roll(section, GY, 1)
    stacked = jnp.concatenate([section, turned_section], axis=0)
    stacked_high, stacked_low = split(stacked)
    both = dot(forward_x[0], jnp.concatenate([stacked_high, stacked_low], axis=1))
    spec = both[:, :LANES] + both[:, LANES:] + dot(forward_x[1], stacked_high)
    spec_turned = pltpu.roll(spec, GY, 1)
    spec3, spec3_turned = spec.reshape(SHOTS, grid_x, LANES), spec_turned.reshape(SHOTS, grid_x, LANES)
    for p in range(2):
        shifted = [
            (spec3 * shift[k, 0][None] + spec3_turned * shift[k, 1][None]).reshape(half, LANES) for k in (2 * p, 2 * p + 1)
        ]
        back = dot3(jnp.concatenate(shifted, axis=1), inverse_y[0], inverse_y[1])
        back = jnp.concatenate([back[:, :LANES], back[:, LANES:]], axis=0)
        back_high, back_low = split(back)
        both = dot(inverse_x[0], jnp.concatenate([back_high, back_low], axis=1))
        picture = both[:, :LANES] + both[:, LANES:] + dot(inverse_x[1], back_high)
        energies = jnp.sum((picture * picture).reshape(SHOTS, grid_x, LANES), axis=0)
        for g in range(n_grp):
            energy[g, 2 * p : 2 * p + 2] = energies[2 * g : 2 * g + 2]

    def energy_copy(d):
        target = lax.rem(grp + d, n_grp)
        return pltpu.make_async_remote_copy(
            src_ref=energy.at[target], dst_ref=got_energy.at[d], send_sem=en_send.at[d], recv_sem=en_recv.at[d],
            device_id=device(chip, core, target), device_id_type=MESH,
        )

    for d in range(1, n_grp):
        sends.append(energy_copy(d))
        sends[-1].start()
    image = energy[grp]
    for d in range(1, n_grp):
        energy_copy(d).wait_recv()
        image += got_energy[d]
    n_windows = windows * n_win
    scale = 1.0 / (n_src * grid_x * GY * n_windows * n_windows)
    for p in range(2):
        one, two = image[2 * p : 2 * p + 1] * scale, image[2 * p + 1 : 2 * p + 2] * scale
        low = iota((1, LANES), 1) < GY
        out[2 * p : 2 * p + 1] = jnp.where(low, one, pltpu.roll(two, GY, 1))
        out[2 * p + 1 : 2 * p + 2] = jnp.where(low, pltpu.roll(one, GY, 1), two)

    for copy in sends:
        copy.wait_send()


def body(n_grp, n_win, spectra, freq_bins, slowness, positions):
    freqs, windows, _, block = spectra.shape
    side = math.isqrt(n_grp)
    grid_x = 2 * n_grp
    n_freq = n_win // 2
    rows = 2 * windows
    n_src = SHOTS * n_grp
    receivers = n_grp * block
    hbm, vmem, smem = (pl.BlockSpec(memory_space=m) for m in (pl.ANY, pltpu.VMEM, pltpu.SMEM))
    dma = pltpu.SemaphoreType.DMA
    consts = tables(grid_x)
    image = pl.pallas_call(
        functools.partial(kernel, n_grp, n_win, side, windows),
        out_shape=jax.ShapeDtypeStruct((4, block), F32),
        in_specs=[hbm, vmem, smem, smem] + [vmem] * len(consts),
        out_specs=vmem,
        scratch_shapes=[
            pltpu.VMEM((n_freq, 2, rows, block), BF16),
            pltpu.VMEM((n_freq, 2, rows, block), BF16),
            pltpu.VMEM((n_grp, n_freq * SHOTS, 2 * rows), BF16),
            pltpu.VMEM((n_freq, n_src, 2 * rows), BF16),
            pltpu.VMEM((n_freq, n_src, 2 * block), F32),
            pltpu.VMEM((n_freq, n_src, 2 * block), F32),
            pltpu.VMEM((n_grp, 2 * SHOTS, block), F32),
            pltpu.VMEM((n_grp, 2 * SHOTS, block), F32),
            pltpu.VMEM((n_grp, SHOTS, block), F32),
            pltpu.VMEM((n_grp, SHOTS, block), F32),
            pltpu.VMEM((2 * LANES, receivers), BF16),
            pltpu.VMEM((grid_x, receivers), BF16),
            pltpu.VMEM((4, 2, grid_x, LANES), F32),
            dma((1,)), dma((2,)),
            dma((n_grp,)), dma((n_grp,)), dma((n_freq,)), dma((n_freq,)),
            dma((n_grp,)), dma((n_grp,)), dma((n_grp,)), dma((n_grp,)),
        ],
        compiler_params=pltpu.CompilerParams(
            collective_id=0, has_side_effects=True, vmem_limit_bytes=48 * 1024 * 1024
        ),
    )(
        spectra.reshape(n_freq, 2, rows, block),
        positions.reshape(1, receivers),
        freq_bins,
        slowness,
        *(jnp.asarray(c) for c in consts),
    )
    return image[None]


def solution(mesh):
    return jax.shard_map(
        functools.partial(body, mesh.shape["grp"], mesh.shape["win"]),
        mesh=mesh,
        in_specs=(P(None, "win", None, "grp"), P(), P(), P()),
        out_specs=P("win", None, "grp"),
        check_vma=False,
    )
```

```python
import functools
import math

import jax
import jax.numpy as jnp
import numpy as np
from jax import lax
from jax.experimental import pallas as pl
from jax.experimental.pallas import tpu as pltpu
from jax.sharding import PartitionSpec as P

MESH = pl.DeviceIdType.MESH
GY = 64
N_X = 4
LANES = 128
SHOTS = 4
F32, BF16 = jnp.float32, jnp.bfloat16


def split(table):
    high = table.astype(BF16)
    return high, (table - high.astype(F32)).astype(BF16)


def dot(a, b):
    return jnp.dot(a, b, preferred_element_type=F32)


def dot_lanes(a, b):
    return lax.dot_general(a, b, (((1,), (1,)), ((), ())), preferred_element_type=F32)


def dot3(a, b_high, b_low):
    high, low = split(a)
    width = b_high.shape[1]
    both = dot(high, jnp.concatenate([b_high, b_low], axis=1))
    return both[:, :width] + both[:, width:] + dot(low, b_high)


def np_split(table):
    table = table.astype(np.float32)
    high = table.astype(BF16)
    return high, (table - high.astype(np.float32)).astype(BF16)


def tables(grid_x):
    def angles(length):
        index = np.arange(length)
        return (index[:, None] * index[None, :] % length) * (2.0 * math.pi / length)

    cos_x, sin_x = np.cos(angles(grid_x)), np.sin(angles(grid_x))
    cos_y, sin_y = np.cos(angles(GY)), np.sin(angles(GY))
    shots = np.eye(SHOTS)
    block_cos, block_sin = np.kron(shots, cos_x), np.kron(shots, sin_x)
    rows_y = np.concatenate([cos_y, sin_y], axis=0)
    forward_x = np.concatenate([block_cos, block_sin], axis=1)
    inverse_x = np.concatenate([block_cos, -block_sin], axis=1)
    to_re = np.concatenate([cos_y, -sin_y], axis=0)
    to_im = np.concatenate([sin_y, cos_y], axis=0)
    none = np.zeros_like(to_re)
    inverse_y = np.block([[to_re, none, to_im, none], [none, to_re, none, to_im]])
    x_index, y_index = np.arange(grid_x), np.arange(GY)
    x_signed = np.where(x_index < (grid_x + 1) // 2, x_index, x_index - grid_x).astype(np.float32) * np.float32(
        2.0 * math.pi / grid_x
    )
    y_signed = np.where(y_index < (GY + 1) // 2, y_index, y_index - GY).astype(np.float32) * np.float32(
        2.0 * math.pi / GY
    )
    squares = x_signed[:, None] ** 2 + y_signed[None, :] ** 2
    return (
        np.stack(np_split(rows_y)),
        np.stack(np_split(forward_x)),
        np.stack(np_split(inverse_x)),
        np.stack(np_split(inverse_y)),
        np.concatenate([squares, squares], axis=1).astype(np.float32),
    )


def iota(shape, dim):
    return lax.broadcasted_iota(jnp.int32, shape, dim)


def one_hot(condition):
    return jnp.where(condition, 1.0, 0.0).astype(BF16)


def kernel(
    n_grp, n_win, windows,
    spectra, positions_hbm, freq_hbm, slowness_hbm, rows_hbm, forward_hbm, inverse_x_hbm, inverse_y_hbm, squares_hbm,
    out,
    positions, freq_bins, slowness, rows_y, forward_x, inverse_x, inverse_y, squares,
    u, v, picked, theirs, gram, got_plus, got_minus, got_z, tiles, got_tiles, energy, got_energy,
    y_phase, x_mask, shift,
    local_sem, core_sem, z_send, z_recv, x_send, x_recv, rs_send, rs_recv, zx_sem, aa_send, aa_recv, en_send, en_recv,
):
    n_freq = n_win // 2
    n_y = n_freq // 2
    n_z = n_grp // N_X
    n_src = SHOTS * n_grp
    grid_x = 2 * n_grp
    receivers = n_grp * LANES
    rows = 2 * windows
    win, grp = lax.axis_index("win"), lax.axis_index("grp")
    core, chip = lax.rem(win, 2), lax.div(win, 2)
    z_low, y = lax.rem(chip, 2), lax.div(chip, 2)
    zh, x = lax.rem(grp, n_z), lax.div(grp, n_z)
    other = 1 - core

    def at_y(d):
        return lax.rem(y + d + n_y, n_y)

    def at_x(d):
        return lax.rem(x + d + N_X, N_X)

    def at_zh(d):
        return lax.rem(zh + d + n_z, n_z)

    def device(chip_at, core_at, grp_at):
        return (chip_at * 2 + core_at, grp_at)

    def remote(src, dst, send_sem, recv_sem, target):
        return pltpu.make_async_remote_copy(
            src_ref=src, dst_ref=dst, send_sem=send_sem, recv_sem=recv_sem, device_id=target, device_id_type=MESH
        )

    sends = []

    def send(copy):
        copy.start()
        sends.append(copy)

    partner = device(chip, other, grp)
    z_partner = device(y * 2 + 1 - z_low, core, grp)
    barrier = pltpu.get_barrier_semaphore()
    greeted = [partner, z_partner, device(at_y(1) * 2 + z_low, core, grp), device(at_y(-1) * 2 + z_low, core, grp)]
    greeted += [device(chip, core, lax.rem(grp + d, n_grp)) for d in range(1, n_grp)]
    for target in greeted:
        pl.semaphore_signal(barrier, inc=1, device_id=target, device_id_type=MESH)

    loads = [
        pltpu.make_async_copy(source, target, local_sem.at[i])
        for i, (source, target) in enumerate(
            (
                (spectra.at[:, core], u.at[:, core]),
                (spectra.at[:, other], v),
                (positions_hbm, positions),
                (freq_hbm, freq_bins),
                (slowness_hbm, slowness),
                (rows_hbm, rows_y),
                (forward_hbm, forward_x),
                (inverse_x_hbm, inverse_x),
                (inverse_y_hbm, inverse_y),
                (squares_hbm, squares),
            )
        )
    ]
    for load in loads:
        load.start()

    ahead = [n_y // 2] + [d for k in range(n_y // 2 - 1, 0, -1) for d in (k, -k)] + [0]
    slots = [(d, z) for d in ahead for z in range(2)]
    chunk = 16 // SHOTS
    n_chunk = n_freq // chunk

    def freq_of(slot):
        return at_y(slots[slot][0]) * 2 + slots[slot][1]

    loads[0].wait()
    loads[1].wait()
    row, lane = iota((n_freq * SHOTS, LANES), 0), iota((n_freq * SHOTS, LANES), 1)
    own = jnp.zeros((n_freq * SHOTS, rows), F32)
    for_partner = jnp.zeros((n_freq * SHOTS, rows), F32)
    for slot in range(n_freq):
        pick = one_hot(lane == (row - SHOTS * slot) * (LANES // SHOTS))
        own += dot_lanes(pick, u[freq_of(slot), core])
        for_partner += dot_lanes(pick, v[freq_of(slot)])
    own, for_partner = own.astype(BF16), for_partner.astype(BF16)
    for c in range(n_chunk):
        picked[c, grp, core] = own[16 * c : 16 * c + 16]
        theirs[c] = for_partner[16 * c : 16 * c + 16]

    pl.semaphore_wait(barrier, len(greeted))

    pick_copy = remote(theirs, picked.at[:, grp, core], core_sem.at[0], core_sem.at[1], partner)
    send(pick_copy)
    core_copy = remote(v, u.at[:, core], core_sem.at[2], core_sem.at[3], partner)
    send(core_copy)
    pick_copy.wait_recv()

    def z_copy(c, d, holder):
        return remote(
            picked.at[c, holder], picked.at[c, holder], z_send.at[c, d], z_recv.at[c, d],
            device(chip, core, x * n_z + at_zh(d)),
        )

    def x_copy(c, holder_x, first, count, step, kind):
        part = pl.ds(holder_x * n_z + first, count)
        sem = 2 * kind + (0 if step > 0 else 1)
        return remote(
            picked.at[c, part], picked.at[c, part], x_send.at[c, sem], x_recv.at[c, sem],
            device(chip, core, at_x(step) * n_z + zh),
        )

    for c in range(n_chunk):
        for d in range(1, n_z):
            send(z_copy(c, d, grp))

    def x_start(c):
        for d in range(1, n_z):
            z_copy(c, d, x * n_z + at_zh(-d)).wait_recv()
        for step in (1, -1):
            send(x_copy(c, x, 0, n_z, step, 0))

    def x_forward(c):
        for step in (1, -1):
            x_copy(c, at_x(-step), 0, n_z, step, 0).wait_recv()
            send(x_copy(c, at_x(-step), 0 if step > 0 else n_z // 2, n_z // 2, step, 1))

    def x_finish(c):
        for step in (1, -1):
            x_copy(c, at_x(-2 * step), 0 if step > 0 else n_z // 2, n_z // 2, step, 1).wait_recv()

    def side_tables():
        for load in loads[2:]:
            load.wait()
        where = positions[...]
        cell_x, cell_y = lax.shift_right_logical(where, 6), jnp.bitwise_and(where, GY - 1)
        y_hot = one_hot(iota((GY, receivers), 0) == cell_y)
        y_phase[0:LANES] = dot(rows_y[0], y_hot).astype(BF16)
        y_phase[LANES:] = dot(rows_y[1], y_hot).astype(BF16)
        x_mask[...] = one_hot(iota((grid_x, receivers), 0) == cell_x)
        freq = freq_bins[win].astype(F32)
        sign = jnp.where(iota((grid_x, LANES), 1) < GY, -1.0, 1.0)
        total_re, total_im = None, None
        for k in range(4):
            kappa = freq * slowness[k]
            excess = kappa * kappa - squares[...]
            vertical = jnp.sqrt(jnp.maximum(excess, 0.0))
            damping = jnp.exp(-jnp.sqrt(jnp.maximum(-excess, 0.0)))
            step_re, step_im = damping * jnp.cos(vertical), damping * jnp.sin(vertical)
            if k == 0:
                total_re, total_im = step_re, step_im
            else:
                total_re, total_im = total_re * step_re - total_im * step_im, total_re * step_im + total_im * step_re
            shift[k, 0] = total_re
            shift[k, 1] = sign * total_im

    height = 16 * n_grp
    row, lane = iota((height, height), 0), iota((height, height), 1)
    slot_of, src_of = lax.div(row, n_src), lax.rem(row, n_src)
    reorder = one_hot(lane == lax.div(src_of, SHOTS) * 16 + slot_of * SHOTS + lax.rem(src_of, SHOTS))
    row, lane = iota((rows, rows), 0), iota((rows, rows), 1)
    even = lax.rem(row, 2) == 0
    turn = jnp.where(~even & (lane == row - 1), -1.0, jnp.where(even & (lane == row + 1), 1.0, 0.0)).astype(BF16)

    def grams(c):
        sources = []
        for half in range(2):
            plain = dot(reorder, picked[c, :, half].reshape(height, rows)).astype(BF16)
            sources.append((plain, dot(plain, turn).astype(BF16)))
        for i in range(chunk):
            slot = chunk * c + i
            q = freq_of(slot)
            result = None
            for half, (plain, turned) in enumerate(sources):
                left = jnp.concatenate([plain[n_src * i : n_src * (i + 1)], turned[n_src * i : n_src * (i + 1)]], axis=0)
                term = dot(left, u[q, half])
                result = term if result is None else result + term
            gram[slot] = result

    def ring_copy(d, z, step):
        slot = slots.index((abs(d) if abs(d) == n_y // 2 else d, z))
        index = (abs(d) - 1) * 2 + z
        got = got_plus if step > 0 else got_minus
        lane_ = 0 if step > 0 else 1
        return remote(
            gram.at[slot], got.at[index], rs_send.at[lane_, index], rs_recv.at[lane_, index],
            device(at_y(step) * 2 + z_low, core, grp),
        )

    def ring_start(d, z, step):
        send(ring_copy(d, z, step))

    def arrived(d, z, step):
        ring_copy(d + step, z, step).wait_recv()
        got = got_plus if step > 0 else got_minus
        return got[(abs(d + step) - 1) * 2 + z]

    def ring_forward(d, z, step):
        slot = slots.index((d, z))
        gram[slot] = gram[slot] + arrived(d, z, step)
        ring_start(d, z, step)

    far = n_y // 2

    def ring(c):
        for place in (2 * c - 1, 2 * c):
            if place < 0:
                continue
            d = ahead[place]
            if d == far:
                ring_start(far, 0, 1)
                ring_start(-far, 1, -1)
                ring_start(far - 1, 1, 1)
            elif d > 0:
                if d == far - 1:
                    ring_forward(d, 0, 1)
                else:
                    ring_forward(d, 1, 1)
                    ring_forward(d, 0, 1)
            elif d < 0:
                if d == 1 - far:
                    ring_start(d, 0, -1)
                    ring_forward(d, 1, -1)
                else:
                    ring_forward(d, 0, -1)
                    ring_forward(d, 1, -1)

    for c in range(n_chunk + 2):
        if c < n_chunk:
            x_start(c)
        if c == 0:
            side_tables()
        if 0 <= c - 1 < n_chunk:
            x_forward(c - 1)
        if 0 <= c - 2 < n_chunk:
            x_finish(c - 2)
            if c == 2:
                core_copy.wait_recv()
            grams(c - 2)
            ring(c - 2)
    totals = [gram[slots.index((0, z))] + arrived(0, z, 1) + arrived(0, z, -1) for z in range(2)]
    kept, passed = slots.index((0, 0)), slots.index((0, 1))
    swap = z_low == 0
    gram[kept] = jnp.where(swap, totals[0], totals[1])
    gram[passed] = jnp.where(swap, totals[1], totals[0])
    z_sum = remote(gram.at[passed], got_z, zx_sem.at[0], zx_sem.at[1], z_partner)
    send(z_sum)
    z_sum.wait_recv()
    total = gram[kept] + got_z[...]

    real, imag = total[:n_src], total[n_src:]
    upper = lax.rem(iota((n_src, LANES), 0), 8) < SHOTS
    first = jnp.where(upper, real, pltpu.roll(imag, SHOTS, 0))
    second = jnp.where(upper, pltpu.roll(real, n_src - SHOTS, 0), imag)
    for a in range(n_grp // 2):
        tiles[2 * a] = first[8 * a : 8 * a + 8]
        tiles[2 * a + 1] = second[8 * a : 8 * a + 8]

    def tile_copy(d):
        target = lax.rem(grp + d, n_grp)
        return pltpu.make_async_remote_copy(
            src_ref=tiles.at[target], dst_ref=got_tiles.at[grp], send_sem=aa_send.at[d], recv_sem=aa_recv.at[d],
            device_id=device(chip, core, target), device_id_type=MESH,
        )

    for d in range(1, n_grp):
        sends.append(tile_copy(d))
        sends[-1].start()
    got_tiles[grp] = tiles[grp]
    for d in range(1, n_grp):
        tile_copy(d).wait_recv()

    field = jnp.concatenate([got_tiles[g] for g in range(n_grp)], axis=1)
    field_high = field.astype(BF16).astype(F32)
    field_low = field - field_high
    mask = x_mask[...]

    def placed(part):
        return jnp.concatenate(
            [jnp.broadcast_to(part[i : i + 1], (grid_x, receivers)).astype(BF16) * mask for i in range(2 * SHOTS)], axis=0
        )

    section = dot_lanes(placed(field_high), y_phase[...])
    section = section[:, :LANES] + section[:, LANES:] + dot_lanes(placed(field_low), y_phase[0:LANES])
    half = SHOTS * grid_x
    lower = iota((half, LANES), 1) < GY
    plus_minus = jnp.where(lower, 1.0, -1.0)
    section = plus_minus * section[:half] + pltpu.roll(section[half:], GY, 1)
    turned_section = plus_minus * pltpu.roll(section, GY, 1)
    stacked = jnp.concatenate([section, turned_section], axis=0)
    stacked_high, stacked_low = split(stacked)
    both = dot(forward_x[0], jnp.concatenate([stacked_high, stacked_low], axis=1))
    spec = both[:, :LANES] + both[:, LANES:] + dot(forward_x[1], stacked_high)
    spec_turned = pltpu.roll(spec, GY, 1)
    spec3, spec3_turned = spec.reshape(SHOTS, grid_x, LANES), spec_turned.reshape(SHOTS, grid_x, LANES)
    for p in range(2):
        shifted = [
            (spec3 * shift[k, 0][None] + spec3_turned * shift[k, 1][None]).reshape(half, LANES) for k in (2 * p, 2 * p + 1)
        ]
        back = dot3(jnp.concatenate(shifted, axis=1), inverse_y[0], inverse_y[1])
        back = jnp.concatenate([back[:, :LANES], back[:, LANES:]], axis=0)
        back_high, back_low = split(back)
        both = dot(inverse_x[0], jnp.concatenate([back_high, back_low], axis=1))
        picture = both[:, :LANES] + both[:, LANES:] + dot(inverse_x[1], back_high)
        energies = jnp.sum((picture * picture).reshape(SHOTS, grid_x, LANES), axis=0)
        for g in range(n_grp):
            energy[g, 2 * p : 2 * p + 2] = energies[2 * g : 2 * g + 2]

    def energy_copy(d):
        target = lax.rem(grp + d, n_grp)
        return pltpu.make_async_remote_copy(
            src_ref=energy.at[target], dst_ref=got_energy.at[d], send_sem=en_send.at[d], recv_sem=en_recv.at[d],
            device_id=device(chip, core, target), device_id_type=MESH,
        )

    for d in range(1, n_grp):
        sends.append(energy_copy(d))
        sends[-1].start()
    image = energy[grp]
    for d in range(1, n_grp):
        energy_copy(d).wait_recv()
        image += got_energy[d]
    n_windows = windows * n_win
    scale = 1.0 / (n_src * grid_x * GY * n_windows * n_windows)
    for p in range(2):
        one, two = image[2 * p : 2 * p + 1] * scale, image[2 * p + 1 : 2 * p + 2] * scale
        low = iota((1, LANES), 1) < GY
        out[2 * p : 2 * p + 1] = jnp.where(low, one, pltpu.roll(two, GY, 1))
        out[2 * p + 1 : 2 * p + 2] = jnp.where(low, pltpu.roll(one, GY, 1), two)

    for copy in sends:
        copy.wait_send()


def body(n_grp, n_win, spectra, freq_bins, slowness, positions):
    freqs, windows, _, block = spectra.shape
    grid_x = 2 * n_grp
    n_freq = n_win // 2
    n_chunk = n_freq * SHOTS // 16
    n_z = n_grp // N_X
    rows = 2 * windows
    n_src = SHOTS * n_grp
    receivers = n_grp * block
    hbm = pl.BlockSpec(memory_space=pltpu.HBM)
    dma = pltpu.SemaphoreType.DMA
    consts = tables(grid_x)
    image = pl.pallas_call(
        functools.partial(kernel, n_grp, n_win, windows),
        out_shape=jax.ShapeDtypeStruct((4, block), F32),
        in_specs=[hbm] * (4 + len(consts)),
        out_specs=pl.BlockSpec(memory_space=pltpu.VMEM),
        scratch_shapes=[
            pltpu.VMEM((1, receivers), jnp.int32),
            pltpu.SMEM((n_win,), jnp.int32),
            pltpu.SMEM((4,), F32),
            *(pltpu.VMEM(c.shape, c.dtype) for c in consts),
            pltpu.VMEM((n_freq, 2, rows, block), BF16),
            pltpu.VMEM((n_freq, rows, block), BF16),
            pltpu.VMEM((n_chunk, n_grp, 2, 16, rows), BF16),
            pltpu.VMEM((n_chunk, 16, rows), BF16),
            pltpu.VMEM((n_freq, 2 * n_src, block), F32),
            pltpu.VMEM((n_freq // 2, 2 * n_src, block), F32),
            pltpu.VMEM((n_freq // 2, 2 * n_src, block), F32),
            pltpu.VMEM((2 * n_src, block), F32),
            pltpu.VMEM((n_grp, 2 * SHOTS, block), F32),
            pltpu.VMEM((n_grp, 2 * SHOTS, block), F32),
            pltpu.VMEM((n_grp, SHOTS, block), F32),
            pltpu.VMEM((n_grp, SHOTS, block), F32),
            pltpu.VMEM((2 * LANES, receivers), BF16),
            pltpu.VMEM((grid_x, receivers), BF16),
            pltpu.VMEM((4, 2, grid_x, LANES), F32),
            dma((5 + len(consts),)), dma((4,)),
            dma((n_chunk, n_z)), dma((n_chunk, n_z)), dma((n_chunk, 4)), dma((n_chunk, 4)),
            dma((2, n_freq // 2)), dma((2, n_freq // 2)), dma((2,)),
            dma((n_grp,)), dma((n_grp,)), dma((n_grp,)), dma((n_grp,)),
        ],
        compiler_params=pltpu.CompilerParams(
            collective_id=0, has_side_effects=True, vmem_limit_bytes=63 * 1024 * 1024
        ),
    )(
        spectra.reshape(n_freq, 2, rows, block),
        positions.reshape(1, receivers),
        freq_bins,
        slowness,
        *(jnp.asarray(c) for c in consts),
    )
    return image[None]


def solution(mesh):
    return jax.shard_map(
        functools.partial(body, mesh.shape["grp"], mesh.shape["win"]),
        mesh=mesh,
        in_specs=(P(None, "win", None, "grp"), P(), P(), P()),
        out_specs=P("win", None, "grp"),
        check_vma=False,
    )
```

```python
import functools
import math

import jax
import jax.numpy as jnp
import numpy as np
from jax import lax
from jax.experimental import pallas as pl
from jax.experimental.pallas import tpu as pltpu
from jax.sharding import PartitionSpec as P

MESH = pl.DeviceIdType.MESH
GY = 64
N_X = 4
LANES = 128
SHOTS = 4
F32, BF16 = jnp.float32, jnp.bfloat16


def split(table):
    high = table.astype(BF16)
    return high, (table - high.astype(F32)).astype(BF16)


def dot(a, b):
    return jnp.dot(a, b, preferred_element_type=F32)


def dot_lanes(a, b):
    return lax.dot_general(a, b, (((1,), (1,)), ((), ())), preferred_element_type=F32)


def dot3(a, b_high, b_low):
    high, low = split(a)
    width = b_high.shape[1]
    both = dot(high, jnp.concatenate([b_high, b_low], axis=1))
    return both[:, :width] + both[:, width:] + dot(low, b_high)


CODE_TOP = 32767.0
EXTRA = 16


def coded(block):
    top = jnp.max(jnp.abs(block), axis=0, keepdims=True)
    exponent = jnp.ceil(jnp.log2(jnp.maximum(top, 1e-30)))
    values = jnp.clip(jnp.round(block * (CODE_TOP * jnp.exp2(-exponent))), -CODE_TOP, CODE_TOP)
    return jnp.concatenate([values, jnp.broadcast_to(exponent, (EXTRA, LANES))], axis=0).astype(jnp.int32).astype(jnp.int16)


def decoded(code):
    values = code.astype(jnp.int32).astype(F32)
    rows = code.shape[0] - EXTRA
    return values[:rows] * (jnp.exp2(values[rows : rows + 1]) * (1.0 / CODE_TOP))


def np_split(table):
    table = table.astype(np.float32)
    high = table.astype(BF16)
    return high, (table - high.astype(np.float32)).astype(BF16)


def tables(grid_x):
    def angles(length):
        index = np.arange(length)
        return (index[:, None] * index[None, :] % length) * (2.0 * math.pi / length)

    cos_x, sin_x = np.cos(angles(grid_x)), np.sin(angles(grid_x))
    cos_y, sin_y = np.cos(angles(GY)), np.sin(angles(GY))
    shots = np.eye(SHOTS)
    block_cos, block_sin = np.kron(shots, cos_x), np.kron(shots, sin_x)
    rows_y = np.concatenate([cos_y, sin_y], axis=0)
    forward_x = np.concatenate([block_cos, block_sin], axis=1)
    inverse_x = np.concatenate([block_cos, -block_sin], axis=1)
    to_re = np.concatenate([cos_y, -sin_y], axis=0)
    to_im = np.concatenate([sin_y, cos_y], axis=0)
    none = np.zeros_like(to_re)
    inverse_y = np.block([[to_re, none, to_im, none], [none, to_re, none, to_im]])
    x_index, y_index = np.arange(grid_x), np.arange(GY)
    x_signed = np.where(x_index < (grid_x + 1) // 2, x_index, x_index - grid_x).astype(np.float32) * np.float32(
        2.0 * math.pi / grid_x
    )
    y_signed = np.where(y_index < (GY + 1) // 2, y_index, y_index - GY).astype(np.float32) * np.float32(
        2.0 * math.pi / GY
    )
    squares = x_signed[:, None] ** 2 + y_signed[None, :] ** 2
    return (
        np.stack(np_split(rows_y)),
        np.stack(np_split(forward_x)),
        np.stack(np_split(inverse_x)),
        np.stack(np_split(inverse_y)),
        np.concatenate([squares, squares], axis=1).astype(np.float32),
    )


def iota(shape, dim):
    return lax.broadcasted_iota(jnp.int32, shape, dim)


def one_hot(condition):
    return jnp.where(condition, 1.0, 0.0).astype(BF16)


def kernel(
    n_grp, n_win, windows,
    spectra, positions_hbm, freq_hbm, slowness_hbm, rows_hbm, forward_hbm, inverse_x_hbm, inverse_y_hbm, squares_hbm,
    out,
    positions, freq_bins, slowness, rows_y, forward_x, inverse_x, inverse_y, squares,
    u, v, picked, theirs, own_gram, blocks, got_blocks, tiles, got_tiles, energy, got_energy,
    y_phase, x_mask, shift,
    local_sem, core_sem, z_send, z_recv, x_send, x_recv, rs_send, rs_recv, aa_send, aa_recv, en_send, en_recv,
):
    n_freq = n_win // 2
    n_y = n_freq // 2
    n_z = n_grp // N_X
    n_src = SHOTS * n_grp
    grid_x = 2 * n_grp
    receivers = n_grp * LANES
    rows = 2 * windows
    win, grp = lax.axis_index("win"), lax.axis_index("grp")
    core, chip = lax.rem(win, 2), lax.div(win, 2)
    z_low, y = lax.rem(chip, 2), lax.div(chip, 2)
    zh, x = lax.rem(grp, n_z), lax.div(grp, n_z)
    other = 1 - core

    def at_y(d):
        return lax.rem(y + d + n_y, n_y)

    def at_x(d):
        return lax.rem(x + d + N_X, N_X)

    def at_zh(d):
        return lax.rem(zh + d + n_z, n_z)

    def device(chip_at, core_at, grp_at):
        return (chip_at * 2 + core_at, grp_at)

    def remote(src, dst, send_sem, recv_sem, target):
        return pltpu.make_async_remote_copy(
            src_ref=src, dst_ref=dst, send_sem=send_sem, recv_sem=recv_sem, device_id=target, device_id_type=MESH
        )

    sends = []

    def send(copy):
        copy.start()
        sends.append(copy)

    def hops(offset):
        return min(offset[0], N_X - offset[0]) + 2 * min(offset[1], n_z - offset[1])

    offsets = sorted(((a, b) for a in range(N_X) for b in range(n_z)), key=hops, reverse=True)
    away = offsets[:-1]
    far_z = sorted(range(1, n_z), key=lambda d: -min(d, n_z - d))
    far_x = sorted(range(1, N_X), key=lambda d: -min(d, N_X - d))

    def to(offset):
        return at_x(offset[0]) * n_z + at_zh(offset[1])

    partner = device(chip, other, grp)
    barrier = pltpu.get_barrier_semaphore()
    greeted = [device(chip, core, to(o)) for o in away]
    greeted += [device(lax.rem(chip + d, n_freq), core, grp) for d in range(1, n_freq)] + [partner]
    for target in greeted:
        pl.semaphore_signal(barrier, inc=1, device_id=target, device_id_type=MESH)

    loads = [
        pltpu.make_async_copy(source, target, local_sem.at[i])
        for i, (source, target) in enumerate(
            (
                (spectra.at[:, core], u.at[:, core]),
                (spectra.at[:, other], v),
                (positions_hbm, positions),
                (freq_hbm, freq_bins),
                (slowness_hbm, slowness),
                (rows_hbm, rows_y),
                (forward_hbm, forward_x),
                (inverse_x_hbm, inverse_x),
                (inverse_y_hbm, inverse_y),
                (squares_hbm, squares),
            )
        )
    ]
    for load in loads:
        load.start()

    ahead = [4, 3, -3, 2, 1, -2, -1, 0]
    assert n_y == len(ahead)
    slots = [(d, z) for d in ahead for z in range(2)]
    chunk = 16 // SHOTS
    n_chunk = n_freq // chunk

    def freq_of(slot):
        return at_y(slots[slot][0]) * 2 + slots[slot][1]

    loads[0].wait()
    loads[1].wait()
    row, lane = iota((n_freq * SHOTS, LANES), 0), iota((n_freq * SHOTS, LANES), 1)
    own = jnp.zeros((n_freq * SHOTS, rows), F32)
    for_partner = jnp.zeros((n_freq * SHOTS, rows), F32)
    for slot in range(n_freq):
        pick = one_hot(lane == (row - SHOTS * slot) * (LANES // SHOTS))
        own += dot_lanes(pick, u[freq_of(slot), core])
        for_partner += dot_lanes(pick, v[freq_of(slot)])
    own, for_partner = own.astype(BF16), for_partner.astype(BF16)
    for c in range(n_chunk):
        picked[c, x, zh, core] = own[16 * c : 16 * c + 16]
        theirs[c] = for_partner[16 * c : 16 * c + 16]

    pl.semaphore_wait(barrier, len(greeted))

    pick_copy = remote(theirs, picked.at[:, x, zh, core], core_sem.at[0], core_sem.at[1], partner)
    send(pick_copy)
    core_copy = remote(v, u.at[:, core], core_sem.at[2], core_sem.at[3], partner)
    send(core_copy)
    pick_copy.wait_recv()

    mixed = n_chunk - 2

    def z_copy(c, d, from_zh):
        part = picked.at[c, :, from_zh] if c == mixed else picked.at[c, x, from_zh]
        return remote(part, part, z_send.at[c, d], z_recv.at[c, d], device(chip, core, x * n_z + at_zh(d)))

    def x_copy(c, d, from_x):
        part = picked.at[c, from_x, zh] if c == mixed else picked.at[c, from_x]
        return remote(part, part, x_send.at[c, d], x_recv.at[c, d], device(chip, core, at_x(d) * n_z + zh))

    def z_start(c):
        for d in far_z:
            send(z_copy(c, d, zh))

    def x_start(c):
        for d in far_x:
            send(x_copy(c, d, x))

    def z_wait(c):
        for d in reversed(far_z):
            z_copy(c, d, at_zh(-d)).wait_recv()

    def x_wait(c):
        for d in reversed(far_x):
            x_copy(c, d, at_x(-d)).wait_recv()

    legs = [(x_start, x_wait, z_start, z_wait) if c == mixed else (z_start, z_wait, x_start, x_wait) for c in range(n_chunk)]
    early = [0, mixed] + [c for c in range(1, n_chunk) if c != mixed] if mixed else list(range(n_chunk))
    for c in early:
        legs[c][0](c)

    def side_tables():
        for load in loads[2:]:
            load.wait()
        where = positions[...]
        cell_x, cell_y = lax.shift_right_logical(where, 6), jnp.bitwise_and(where, GY - 1)
        y_hot = one_hot(iota((GY, receivers), 0) == cell_y)
        y_phase[0:LANES] = dot(rows_y[0], y_hot).astype(BF16)
        y_phase[LANES:] = dot(rows_y[1], y_hot).astype(BF16)
        x_mask[...] = one_hot(iota((grid_x, receivers), 0) == cell_x)
        freq = freq_bins[win].astype(F32)
        sign = jnp.where(iota((grid_x, LANES), 1) < GY, -1.0, 1.0)
        total_re, total_im = None, None
        for k in range(4):
            kappa = freq * slowness[k]
            excess = kappa * kappa - squares[...]
            vertical = jnp.sqrt(jnp.maximum(excess, 0.0))
            damping = jnp.exp(-jnp.sqrt(jnp.maximum(-excess, 0.0)))
            step_re, step_im = damping * jnp.cos(vertical), damping * jnp.sin(vertical)
            if k == 0:
                total_re, total_im = step_re, step_im
            else:
                total_re, total_im = total_re * step_re - total_im * step_im, total_re * step_im + total_im * step_re
            shift[k, 0] = total_re
            shift[k, 1] = sign * total_im

    height = 16 * n_grp
    row, lane = iota((height, height), 0), iota((height, height), 1)
    slot_of, src_of = lax.div(row, n_src), lax.rem(row, n_src)
    reorder = one_hot(lane == lax.div(src_of, SHOTS) * 16 + slot_of * SHOTS + lax.rem(src_of, SHOTS))
    row, lane = iota((rows, rows), 0), iota((rows, rows), 1)
    even = lax.rem(row, 2) == 0
    turn = jnp.where(~even & (lane == row - 1), -1.0, jnp.where(even & (lane == row + 1), 1.0, 0.0)).astype(BF16)

    def grams(c):
        sources = []
        for half in range(2):
            plain = dot(reorder, picked[c, :, :, half].reshape(height, rows)).astype(BF16)
            sources.append((plain, dot(plain, turn).astype(BF16)))
        first_here = None
        for i in range(chunk):
            slot = chunk * c + i
            q = freq_of(slot)
            result = None
            for half, (plain, turned) in enumerate(sources):
                left = jnp.concatenate([plain[n_src * i : n_src * (i + 1)], turned[n_src * i : n_src * (i + 1)]], axis=0)
                term = dot(left, u[q, half])
                result = term if result is None else result + term
            d, z = slots[slot]
            if abs(d) == 2:
                for passed in ((2 * d, 3 * d // 2) if (d > 0) == (z == 0) else (3 * d // 2,)):
                    result += block_arrived(slots.index((abs(passed) if passed == -4 else passed, z)))
            if d:
                block_send(slot, result)
            elif z == 0:
                first_here = result
            else:
                here = z_low == 0
                own_gram[...] = jnp.where(here, first_here, result)
                block_send(slot, jnp.where(here, result, first_here))

    def block_copy(slot):
        d, z = slots[slot]
        if abs(d) > 2:
            step = (2 if z == 0 else -2) if d == 4 else d // 3
            target, index = at_y(step) * 2 + z_low, slot
        else:
            target = at_y(d) * 2 + (z if d else 1 - z_low)
            index = slot - slot % 2 + z_low
        return remote(
            blocks.at[slot], got_blocks.at[index], rs_send.at[slot], rs_recv.at[index], device(target, core, grp)
        )

    def block_send(slot, value):
        blocks[slot] = coded(value)
        send(block_copy(slot))

    def block_arrived(index):
        remote(
            blocks.at[0], got_blocks.at[index], rs_send.at[0], rs_recv.at[index], device(at_y(1) * 2 + z_low, core, grp)
        ).wait_recv()
        return decoded(got_blocks[index])

    side_tables()
    for c in early:
        legs[c][1](c)
        legs[c][2](c)
    core_copy.wait_recv()
    for c in range(n_chunk):
        legs[c][3](c)
        grams(c)
    total = own_gram[...]
    for index in range(6, n_freq - 2):
        total += block_arrived(index)
    total += block_arrived(n_freq - 1 - z_low)

    upper = lax.rem(iota((n_src, LANES), 0), 8) < SHOTS
    real, imag = total[:n_src], total[n_src:]
    first = jnp.where(upper, real, pltpu.roll(imag, SHOTS, 0))
    second = jnp.where(upper, pltpu.roll(real, n_src - SHOTS, 0), imag)
    for a in range(n_grp // 2):
        tiles[2 * a] = first[8 * a : 8 * a + 8]
        tiles[2 * a + 1] = second[8 * a : 8 * a + 8]

    def tile_copy(i):
        target = to(away[i])
        return remote(
            tiles.at[target], got_tiles.at[grp], aa_send.at[i], aa_recv.at[i], device(chip, core, target)
        )

    for i in range(n_grp - 1):
        send(tile_copy(i))
    got_tiles[grp] = tiles[grp]
    for i in reversed(range(n_grp - 1)):
        tile_copy(i).wait_recv()

    field = jnp.concatenate([got_tiles[g] for g in range(n_grp)], axis=1)
    field_high = field.astype(BF16).astype(F32)
    field_low = field - field_high
    mask = x_mask[...]

    def placed(part):
        return jnp.concatenate(
            [jnp.broadcast_to(part[i : i + 1], (grid_x, receivers)).astype(BF16) * mask for i in range(2 * SHOTS)], axis=0
        )

    section = dot_lanes(placed(field_high), y_phase[...])
    section = section[:, :LANES] + section[:, LANES:] + dot_lanes(placed(field_low), y_phase[0:LANES])
    half = SHOTS * grid_x
    lower = iota((half, LANES), 1) < GY
    plus_minus = jnp.where(lower, 1.0, -1.0)
    section = plus_minus * section[:half] + pltpu.roll(section[half:], GY, 1)
    turned_section = plus_minus * pltpu.roll(section, GY, 1)
    stacked = jnp.concatenate([section, turned_section], axis=0)
    stacked_high, stacked_low = split(stacked)
    both = dot(forward_x[0], jnp.concatenate([stacked_high, stacked_low], axis=1))
    spec = both[:, :LANES] + both[:, LANES:] + dot(forward_x[1], stacked_high)
    spec_turned = pltpu.roll(spec, GY, 1)
    spec3, spec3_turned = spec.reshape(SHOTS, grid_x, LANES), spec_turned.reshape(SHOTS, grid_x, LANES)
    for p in range(2):
        shifted = [
            (spec3 * shift[k, 0][None] + spec3_turned * shift[k, 1][None]).reshape(half, LANES) for k in (2 * p, 2 * p + 1)
        ]
        back = dot3(jnp.concatenate(shifted, axis=1), inverse_y[0], inverse_y[1])
        back = jnp.concatenate([back[:, :LANES], back[:, LANES:]], axis=0)
        back_high, back_low = split(back)
        both = dot(inverse_x[0], jnp.concatenate([back_high, back_low], axis=1))
        picture = both[:, :LANES] + both[:, LANES:] + dot(inverse_x[1], back_high)
        energies = jnp.sum((picture * picture).reshape(SHOTS, grid_x, LANES), axis=0)
        for g in range(n_grp):
            energy[g, 2 * p : 2 * p + 2] = energies[2 * g : 2 * g + 2]

    def energy_copy(i):
        target = to(away[i])
        return remote(
            energy.at[target], got_energy.at[i], en_send.at[i], en_recv.at[i], device(chip, core, target)
        )

    for i in range(n_grp - 1):
        send(energy_copy(i))
    image = energy[grp]
    for i in reversed(range(n_grp - 1)):
        energy_copy(i).wait_recv()
        image += got_energy[i]
    n_windows = windows * n_win
    scale = 1.0 / (n_src * grid_x * GY * n_windows * n_windows)
    for p in range(2):
        one, two = image[2 * p : 2 * p + 1] * scale, image[2 * p + 1 : 2 * p + 2] * scale
        low = iota((1, LANES), 1) < GY
        out[2 * p : 2 * p + 1] = jnp.where(low, one, pltpu.roll(two, GY, 1))
        out[2 * p + 1 : 2 * p + 2] = jnp.where(low, pltpu.roll(one, GY, 1), two)

    for copy in sends:
        copy.wait_send()


def body(n_grp, n_win, spectra, freq_bins, slowness, positions):
    freqs, windows, _, block = spectra.shape
    grid_x = 2 * n_grp
    n_freq = n_win // 2
    n_chunk = n_freq * SHOTS // 16
    n_z = n_grp // N_X
    rows = 2 * windows
    n_src = SHOTS * n_grp
    receivers = n_grp * block
    hbm = pl.BlockSpec(memory_space=pltpu.HBM)
    dma = pltpu.SemaphoreType.DMA
    consts = tables(grid_x)
    image = pl.pallas_call(
        functools.partial(kernel, n_grp, n_win, windows),
        out_shape=jax.ShapeDtypeStruct((4, block), F32),
        in_specs=[hbm] * (4 + len(consts)),
        out_specs=pl.BlockSpec(memory_space=pltpu.VMEM),
        scratch_shapes=[
            pltpu.VMEM((1, receivers), jnp.int32),
            pltpu.SMEM((n_win,), jnp.int32),
            pltpu.SMEM((4,), F32),
            *(pltpu.VMEM(c.shape, c.dtype) for c in consts),
            pltpu.VMEM((n_freq, 2, rows, block), BF16),
            pltpu.VMEM((n_freq, rows, block), BF16),
            pltpu.VMEM((n_chunk, N_X, n_z, 2, 16, rows), BF16),
            pltpu.VMEM((n_chunk, 16, rows), BF16),
            pltpu.VMEM((2 * n_src, block), F32),
            pltpu.VMEM((n_freq, 2 * n_src + EXTRA, block), jnp.int16),
            pltpu.VMEM((n_freq, 2 * n_src + EXTRA, block), jnp.int16),
            pltpu.VMEM((n_grp, 2 * SHOTS, block), F32),
            pltpu.VMEM((n_grp, 2 * SHOTS, block), F32),
            pltpu.VMEM((n_grp, SHOTS, block), F32),
            pltpu.VMEM((n_grp, SHOTS, block), F32),
            pltpu.VMEM((2 * LANES, receivers), BF16),
            pltpu.VMEM((grid_x, receivers), BF16),
            pltpu.VMEM((4, 2, grid_x, LANES), F32),
            dma((5 + len(consts),)), dma((4,)),
            dma((n_chunk, n_z)), dma((n_chunk, n_z)), dma((n_chunk, N_X)), dma((n_chunk, N_X)),
            dma((n_freq,)), dma((n_freq,)),
            dma((n_grp,)), dma((n_grp,)), dma((n_grp,)), dma((n_grp,)),
        ],
        compiler_params=pltpu.CompilerParams(
            collective_id=0, has_side_effects=True, vmem_limit_bytes=63 * 1024 * 1024
        ),
    )(
        spectra.reshape(n_freq, 2, rows, block),
        positions.reshape(1, receivers),
        freq_bins,
        slowness,
        *(jnp.asarray(c) for c in consts),
    )
    return image[None]


def solution(mesh):
    return jax.shard_map(
        functools.partial(body, mesh.shape["grp"], mesh.shape["win"]),
        mesh=mesh,
        in_specs=(P(None, "win", None, "grp"), P(), P(), P()),
        out_specs=P("win", None, "grp"),
        check_vma=False,
    )
```

```python
import functools
import math

import jax
import jax.numpy as jnp
import numpy as np
from jax import lax
from jax.experimental import pallas as pl
from jax.experimental.pallas import tpu as pltpu
from jax.sharding import PartitionSpec as P

MESH = pl.DeviceIdType.MESH
GY = 64
N_X = 4
LANES = 128
SHOTS = 4
F32, BF16 = jnp.float32, jnp.bfloat16


def split(table):
    high = table.astype(BF16)
    return high, (table - high.astype(F32)).astype(BF16)


def dot(a, b):
    return jnp.dot(a, b, preferred_element_type=F32)


def dot_lanes(a, b):
    return lax.dot_general(a, b, (((1,), (1,)), ((), ())), preferred_element_type=F32)


def dot3(a, b_high, b_low):
    high, low = split(a)
    width = b_high.shape[1]
    both = dot(high, jnp.concatenate([b_high, b_low], axis=1))
    return both[:, :width] + both[:, width:] + dot(low, b_high)


CODE_TOP = 32767.0
EXTRA = 16


def coded(block):
    top = jnp.max(jnp.abs(block), axis=0, keepdims=True)
    exponent = jnp.ceil(jnp.log2(jnp.maximum(top, 1e-30)))
    values = jnp.clip(jnp.round(block * (CODE_TOP * jnp.exp2(-exponent))), -CODE_TOP, CODE_TOP)
    return jnp.concatenate([values, jnp.broadcast_to(exponent, (EXTRA, LANES))], axis=0).astype(jnp.int32).astype(jnp.int16)


def decoded(code):
    values = code.astype(jnp.int32).astype(F32)
    rows = code.shape[0] - EXTRA
    return values[:rows] * (jnp.exp2(values[rows : rows + 1]) * (1.0 / CODE_TOP))


def np_split(table):
    table = table.astype(np.float32)
    high = table.astype(BF16)
    return high, (table - high.astype(np.float32)).astype(BF16)


def tables(grid_x):
    def angles(length):
        index = np.arange(length)
        return (index[:, None] * index[None, :] % length) * (2.0 * math.pi / length)

    cos_x, sin_x = np.cos(angles(grid_x)), np.sin(angles(grid_x))
    cos_y, sin_y = np.cos(angles(GY)), np.sin(angles(GY))
    shots = np.eye(SHOTS)
    block_cos, block_sin = np.kron(shots, cos_x), np.kron(shots, sin_x)
    rows_y = np.concatenate([cos_y, sin_y], axis=0)
    forward_x = np.concatenate([block_cos, block_sin], axis=1)
    inverse_x = np.concatenate([block_cos, -block_sin], axis=1)
    to_re = np.concatenate([cos_y, -sin_y], axis=0)
    to_im = np.concatenate([sin_y, cos_y], axis=0)
    none = np.zeros_like(to_re)
    inverse_y = np.block([[to_re, none, to_im, none], [none, to_re, none, to_im]])
    x_index, y_index = np.arange(grid_x), np.arange(GY)
    x_signed = np.where(x_index < (grid_x + 1) // 2, x_index, x_index - grid_x).astype(np.float32) * np.float32(
        2.0 * math.pi / grid_x
    )
    y_signed = np.where(y_index < (GY + 1) // 2, y_index, y_index - GY).astype(np.float32) * np.float32(
        2.0 * math.pi / GY
    )
    squares = x_signed[:, None] ** 2 + y_signed[None, :] ** 2
    return (
        np.stack(np_split(rows_y)),
        np.stack(np_split(forward_x)),
        np.stack(np_split(inverse_x)),
        np.stack(np_split(inverse_y)),
        np.concatenate([squares, squares], axis=1).astype(np.float32),
    )


def iota(shape, dim):
    return lax.broadcasted_iota(jnp.int32, shape, dim)


def one_hot(condition):
    return jnp.where(condition, 1.0, 0.0).astype(BF16)


def kernel(
    n_grp, n_win, windows,
    spectra, positions_hbm, freq_hbm, slowness_hbm, rows_hbm, forward_hbm, inverse_x_hbm, inverse_y_hbm, squares_hbm,
    out,
    positions, freq_bins, slowness, rows_y, forward_x, inverse_x, inverse_y, squares,
    u, v, picked, theirs, own_gram, blocks, got_blocks, tiles, got_tiles, energy, got_energy,
    y_phase, x_mask, shift,
    local_sem, core_sem, pick_send, pick_recv, first_send, first_recv, second_send, second_recv, rs_send, rs_recv, tile_sem, energy_sem,
):
    n_freq = n_win // 2
    n_y = n_freq // 2
    n_z = n_grp // N_X
    n_src = SHOTS * n_grp
    grid_x = 2 * n_grp
    receivers = n_grp * LANES
    rows = 2 * windows
    win, grp = lax.axis_index("win"), lax.axis_index("grp")
    core, chip = lax.rem(win, 2), lax.div(win, 2)
    z_low, y = lax.rem(chip, 2), lax.div(chip, 2)
    zh, x = lax.rem(grp, n_z), lax.div(grp, n_z)
    other = 1 - core

    def at_y(d):
        return lax.rem(y + d + n_y, n_y)

    def at_x(d):
        return lax.rem(x + d + N_X, N_X)

    def at_zh(d):
        return lax.rem(zh + d + n_z, n_z)

    def device(chip_at, core_at, grp_at):
        return (chip_at * 2 + core_at, grp_at)

    def remote(src, dst, send_sem, recv_sem, target):
        return pltpu.make_async_remote_copy(
            src_ref=src, dst_ref=dst, send_sem=send_sem, recv_sem=recv_sem, device_id=target, device_id_type=MESH
        )

    ends = []

    def send(copy):
        copy.start()
        ends.append(copy)

    def send_all(copies, whole):
        for copy in copies:
            copy.start()
        ends.append(whole)

    def drain():
        for copy in ends:
            copy.wait_send()
        ends.clear()

    def hops(offset):
        return min(offset[0], N_X - offset[0]) + 2 * min(offset[1], n_z - offset[1])

    offsets = sorted(((a, b) for a in range(N_X) for b in range(n_z)), key=hops, reverse=True)
    away = offsets[:-1]
    far_z = sorted(range(1, n_z), key=lambda d: -min(d, n_z - d))
    far_x = sorted(range(1, N_X), key=lambda d: -min(d, N_X - d))

    def to(offset):
        return at_x(offset[0]) * n_z + at_zh(offset[1])

    partner = device(chip, other, grp)
    loads = [
        pltpu.make_async_copy(source, target, local_sem.at[i])
        for i, (source, target) in enumerate(
            (
                (spectra.at[:, core], u.at[:, core]),
                (spectra.at[:, other], v),
                (positions_hbm, positions),
                (freq_hbm, freq_bins),
                (slowness_hbm, slowness),
                (rows_hbm, rows_y),
                (forward_hbm, forward_x),
                (inverse_x_hbm, inverse_x),
                (inverse_y_hbm, inverse_y),
                (squares_hbm, squares),
            )
        )
    ]
    for load in loads:
        load.start()

    barrier = pltpu.get_barrier_semaphore()
    greeted = [device(chip, core, to(o)) for o in away]
    greeted += [device(at_y(d) * 2 + z, core, grp) for d in (2, -2, 1, -1) for z in range(2)]
    greeted += [device(y * 2 + 1 - z_low, core, grp), partner]
    greeted += [device(chip, other, to(o)) for o in away if 0 in o]
    for target in greeted:
        pl.semaphore_signal(barrier, inc=1, device_id=target, device_id_type=MESH)

    ahead = [4, 3, -3, 2, 1, -2, -1, 0]
    assert n_y == len(ahead)
    slots = [(d, z) for d in ahead for z in range(2)]
    chunk = 16 // SHOTS
    n_chunk = n_freq // chunk

    def freq_of(slot):
        return at_y(slots[slot][0]) * 2 + slots[slot][1]

    loads[0].wait()
    loads[1].wait()
    row, lane = iota((n_freq * SHOTS, LANES), 0), iota((n_freq * SHOTS, LANES), 1)
    own = jnp.zeros((n_freq * SHOTS, rows), F32)
    for_partner = jnp.zeros((n_freq * SHOTS, rows), F32)
    for slot in range(n_freq):
        pick = one_hot(lane == (row - SHOTS * slot) * (LANES // SHOTS))
        own += dot_lanes(pick, u[freq_of(slot), core])
        for_partner += dot_lanes(pick, v[freq_of(slot)])
    own, for_partner = own.astype(BF16), for_partner.astype(BF16)
    for c in range(n_chunk):
        picked[c, x, 0, core] = own[16 * c : 16 * c + 16]
        theirs[c] = for_partner[16 * c : 16 * c + 16]

    pl.semaphore_wait(barrier, len(greeted))

    mixed = n_chunk - 2

    def first_copy(c, axis, d, to_core):
        peer = to((d, 0) if axis == 0 else (0, d))
        source = picked.at[c, x, 0, core] if to_core == 0 else theirs.at[c]
        return remote(
            source, picked.at[c, x, (n_z - d) % n_z if axis else 0, core], first_send.at[c, axis], first_recv.at[c, axis],
            device(chip, other if to_core else core, peer),
        )

    def first_whole(c, axis):
        part = picked.at[c, x, 1:] if axis else picked.at[c, 1:, 0]
        return remote(part, part, first_send.at[c, axis], first_recv.at[c, axis], partner)

    def first_start(c, axis):
        send_all(
            [first_copy(c, axis, d, to_core) for d in (far_z if axis else far_x) for to_core in range(2)],
            first_whole(c, axis),
        )

    def second_copy(c, d):
        if c == mixed:
            source, target, offset = picked.at[c, :, 0], picked.at[c, :, n_z - d], (0, d)
        else:
            source, target, offset = picked.at[c, x, 1:], picked.at[c, x, 1:], (d, 0)
        return remote(source, target, second_send.at[c], second_recv.at[c], device(chip, core, to(offset)))

    def second_whole(c):
        part = picked.at[c, :, 1:] if c == mixed else picked.at[c, 1:, 1:]
        return remote(part, part, second_send.at[c], second_recv.at[c], partner)

    def second_start(c):
        send_all([second_copy(c, d) for d in (far_z if c == mixed else far_x)], second_whole(c))

    def second_wait(c):
        second_whole(c).wait_recv()
        if c != mixed:
            first_whole(c, 0).wait_recv()

    pick_copies = [
        remote(theirs.at[c], picked.at[c, x, 0, core], pick_send.at[c], pick_recv.at[c], partner) for c in range(n_chunk)
    ]
    core_copy = remote(v, u.at[:, core], core_sem.at[0], core_sem.at[1], partner)
    early = [0, mixed] + [c for c in range(1, n_chunk) if c != mixed]
    for c in early:
        send(pick_copies[c])
        first_start(c, 0 if c == mixed else 1)
    for c in range(n_chunk):
        if c != mixed:
            first_start(c, 0)
    send(core_copy)

    def side_tables():
        for load in loads[2:]:
            load.wait()
        where = positions[...]
        cell_x, cell_y = lax.shift_right_logical(where, 6), jnp.bitwise_and(where, GY - 1)
        y_hot = one_hot(iota((GY, receivers), 0) == cell_y)
        y_phase[0:LANES] = dot(rows_y[0], y_hot).astype(BF16)
        y_phase[LANES:] = dot(rows_y[1], y_hot).astype(BF16)
        x_mask[...] = one_hot(iota((grid_x, receivers), 0) == cell_x)
        freq = freq_bins[win].astype(F32)
        sign = jnp.where(iota((grid_x, LANES), 1) < GY, -1.0, 1.0)
        total_re, total_im = None, None
        for k in range(4):
            kappa = freq * slowness[k]
            excess = kappa * kappa - squares[...]
            vertical = jnp.sqrt(jnp.maximum(excess, 0.0))
            damping = jnp.exp(-jnp.sqrt(jnp.maximum(-excess, 0.0)))
            step_re, step_im = damping * jnp.cos(vertical), damping * jnp.sin(vertical)
            if k == 0:
                total_re, total_im = step_re, step_im
            else:
                total_re, total_im = total_re * step_re - total_im * step_im, total_re * step_im + total_im * step_re
            shift[k, 0] = total_re
            shift[k, 1] = sign * total_im

    height = 16 * n_grp
    row, lane = iota((height, height), 0), iota((height, height), 1)
    slot_of, src_of = lax.div(row, n_src), lax.rem(row, n_src)
    origin = lax.div(src_of, SHOTS)
    held = lax.div(origin, n_z) * n_z + lax.rem(lax.rem(origin, n_z) + n_z - zh, n_z)
    reorder = one_hot(lane == held * 16 + slot_of * SHOTS + lax.rem(src_of, SHOTS))
    row, lane = iota((rows, rows), 0), iota((rows, rows), 1)
    even = lax.rem(row, 2) == 0
    turn = jnp.where(~even & (lane == row - 1), -1.0, jnp.where(even & (lane == row + 1), 1.0, 0.0)).astype(BF16)

    def grams(c):
        sources = []
        for half in range(2):
            plain = dot(reorder, picked[c, :, :, half].reshape(height, rows)).astype(BF16)
            sources.append((plain, dot(plain, turn).astype(BF16)))
        first_here = None
        for i in range(chunk):
            slot = chunk * c + i
            q = freq_of(slot)
            result = None
            for half, (plain, turned) in enumerate(sources):
                left = jnp.concatenate([plain[n_src * i : n_src * (i + 1)], turned[n_src * i : n_src * (i + 1)]], axis=0)
                term = dot(left, u[q, half])
                result = term if result is None else result + term
            d, z = slots[slot]
            if abs(d) == 2:
                for passed in ((2 * d, 3 * d // 2) if (d > 0) == (z == 0) else (3 * d // 2,)):
                    result += block_arrived(slots.index((abs(passed) if passed == -4 else passed, z)))
            if d:
                block_send(slot, result)
            elif z == 0:
                first_here = result
            else:
                here = z_low == 0
                own_gram[...] = jnp.where(here, first_here, result)
                block_send(slot, jnp.where(here, result, first_here))

    def block_copy(slot):
        d, z = slots[slot]
        if abs(d) > 2:
            step = (2 if z == 0 else -2) if d == 4 else d // 3
            target, index = at_y(step) * 2 + z_low, slot
        else:
            target = at_y(d) * 2 + (z if d else 1 - z_low)
            index = slot - slot % 2 + z_low
        return remote(
            blocks.at[slot], got_blocks.at[index], rs_send.at[slot], rs_recv.at[index], device(target, core, grp)
        )

    def block_send(slot, value):
        blocks[slot] = coded(value)
        send(block_copy(slot))

    def block_arrived(index):
        remote(
            blocks.at[0], got_blocks.at[index], rs_send.at[0], rs_recv.at[index], device(at_y(1) * 2 + z_low, core, grp)
        ).wait_recv()
        return decoded(got_blocks[index])

    side_tables()
    for c in early:
        pick_copies[c].wait_recv()
        first_whole(c, 0 if c == mixed else 1).wait_recv()
        second_start(c)
    core_copy.wait_recv()
    for c in range(n_chunk):
        second_wait(c)
        grams(c)
    total = own_gram[...]
    for index in range(6, n_freq - 2):
        total += block_arrived(index)
    total += block_arrived(n_freq - 1 - z_low)

    upper = lax.rem(iota((n_src, LANES), 0), 8) < SHOTS
    real, imag = total[:n_src], total[n_src:]
    first = jnp.where(upper, real, pltpu.roll(imag, SHOTS, 0))
    second = jnp.where(upper, pltpu.roll(real, n_src - SHOTS, 0), imag)
    for a in range(n_grp // 2):
        tiles[2 * a] = first[8 * a : 8 * a + 8]
        tiles[2 * a + 1] = second[8 * a : 8 * a + 8]

    def tile_copy(offset):
        target = to(offset)
        return remote(
            tiles.at[target], got_tiles.at[grp], tile_sem.at[0], tile_sem.at[1], device(chip, core, target)
        )

    tiles_whole = remote(tiles.at[1:], got_tiles.at[1:], tile_sem.at[0], tile_sem.at[1], partner)
    got_tiles[grp] = tiles[grp]
    before = list(ends)
    ends.clear()
    send_all([tile_copy(o) for o in away], tiles_whole)
    for copy in before:
        copy.wait_send()
    tiles_whole.wait_recv()

    field = jnp.concatenate([got_tiles[g] for g in range(n_grp)], axis=1)
    field_high = field.astype(BF16).astype(F32)
    field_low = field - field_high
    mask = x_mask[...]

    def placed(part):
        return jnp.concatenate(
            [jnp.broadcast_to(part[i : i + 1], (grid_x, receivers)).astype(BF16) * mask for i in range(2 * SHOTS)], axis=0
        )

    section = dot_lanes(placed(field_high), y_phase[...])
    section = section[:, :LANES] + section[:, LANES:] + dot_lanes(placed(field_low), y_phase[0:LANES])
    half = SHOTS * grid_x
    lower = iota((half, LANES), 1) < GY
    plus_minus = jnp.where(lower, 1.0, -1.0)
    section = plus_minus * section[:half] + pltpu.roll(section[half:], GY, 1)
    turned_section = plus_minus * pltpu.roll(section, GY, 1)
    stacked = jnp.concatenate([section, turned_section], axis=0)
    stacked_high, stacked_low = split(stacked)
    both = dot(forward_x[0], jnp.concatenate([stacked_high, stacked_low], axis=1))
    spec = both[:, :LANES] + both[:, LANES:] + dot(forward_x[1], stacked_high)
    spec_turned = pltpu.roll(spec, GY, 1)
    spec3, spec3_turned = spec.reshape(SHOTS, grid_x, LANES), spec_turned.reshape(SHOTS, grid_x, LANES)
    for p in range(2):
        shifted = [
            (spec3 * shift[k, 0][None] + spec3_turned * shift[k, 1][None]).reshape(half, LANES) for k in (2 * p, 2 * p + 1)
        ]
        back = dot3(jnp.concatenate(shifted, axis=1), inverse_y[0], inverse_y[1])
        back = jnp.concatenate([back[:, :LANES], back[:, LANES:]], axis=0)
        back_high, back_low = split(back)
        both = dot(inverse_x[0], jnp.concatenate([back_high, back_low], axis=1))
        picture = both[:, :LANES] + both[:, LANES:] + dot(inverse_x[1], back_high)
        energies = jnp.sum((picture * picture).reshape(SHOTS, grid_x, LANES), axis=0)
        for g in range(n_grp):
            energy[g, 2 * p : 2 * p + 2] = energies[2 * g : 2 * g + 2]

    def energy_copy(i):
        target = to(away[i])
        return remote(
            energy.at[target], got_energy.at[i], energy_sem.at[0], energy_sem.at[1], device(chip, core, target)
        )

    energy_whole = remote(energy.at[1:], got_energy.at[: n_grp - 1], energy_sem.at[0], energy_sem.at[1], partner)
    send_all([energy_copy(i) for i in range(n_grp - 1)], energy_whole)
    image = energy[grp]
    energy_whole.wait_recv()
    for i in range(n_grp - 1):
        image += got_energy[i]
    n_windows = windows * n_win
    scale = 1.0 / (n_src * grid_x * GY * n_windows * n_windows)
    for p in range(2):
        one, two = image[2 * p : 2 * p + 1] * scale, image[2 * p + 1 : 2 * p + 2] * scale
        low = iota((1, LANES), 1) < GY
        out[2 * p : 2 * p + 1] = jnp.where(low, one, pltpu.roll(two, GY, 1))
        out[2 * p + 1 : 2 * p + 2] = jnp.where(low, pltpu.roll(one, GY, 1), two)

    drain()


def body(n_grp, n_win, spectra, freq_bins, slowness, positions):
    freqs, windows, _, block = spectra.shape
    grid_x = 2 * n_grp
    n_freq = n_win // 2
    n_chunk = n_freq * SHOTS // 16
    n_z = n_grp // N_X
    rows = 2 * windows
    n_src = SHOTS * n_grp
    receivers = n_grp * block
    hbm = pl.BlockSpec(memory_space=pltpu.HBM)
    dma = pltpu.SemaphoreType.DMA
    consts = tables(grid_x)
    image = pl.pallas_call(
        functools.partial(kernel, n_grp, n_win, windows),
        out_shape=jax.ShapeDtypeStruct((4, block), F32),
        in_specs=[hbm] * (4 + len(consts)),
        out_specs=pl.BlockSpec(memory_space=pltpu.VMEM),
        scratch_shapes=[
            pltpu.VMEM((1, receivers), jnp.int32),
            pltpu.SMEM((n_win,), jnp.int32),
            pltpu.SMEM((4,), F32),
            *(pltpu.VMEM(c.shape, c.dtype) for c in consts),
            pltpu.VMEM((n_freq, 2, rows, block), BF16),
            pltpu.VMEM((n_freq, rows, block), BF16),
            pltpu.VMEM((n_chunk, N_X, n_z, 2, 16, rows), BF16),
            pltpu.VMEM((n_chunk, 16, rows), BF16),
            pltpu.VMEM((2 * n_src, block), F32),
            pltpu.VMEM((n_freq, 2 * n_src + EXTRA, block), jnp.int16),
            pltpu.VMEM((n_freq, 2 * n_src + EXTRA, block), jnp.int16),
            pltpu.VMEM((n_grp, 2 * SHOTS, block), F32),
            pltpu.VMEM((n_grp, 2 * SHOTS, block), F32),
            pltpu.VMEM((n_grp, SHOTS, block), F32),
            pltpu.VMEM((n_grp, SHOTS, block), F32),
            pltpu.VMEM((2 * LANES, receivers), BF16),
            pltpu.VMEM((grid_x, receivers), BF16),
            pltpu.VMEM((4, 2, grid_x, LANES), F32),
            dma((5 + len(consts),)), dma((2,)), dma((n_chunk,)), dma((n_chunk,)),
            dma((n_chunk, 2)), dma((n_chunk, 2)), dma((n_chunk,)), dma((n_chunk,)),
            dma((n_freq,)), dma((n_freq,)),
            dma((2,)), dma((2,)),
        ],
        compiler_params=pltpu.CompilerParams(
            collective_id=0, has_side_effects=True, vmem_limit_bytes=63 * 1024 * 1024
        ),
    )(
        spectra.reshape(n_freq, 2, rows, block),
        positions.reshape(1, receivers),
        freq_bins,
        slowness,
        *(jnp.asarray(c) for c in consts),
    )
    return image[None]


def solution(mesh):
    return jax.shard_map(
        functools.partial(body, mesh.shape["grp"], mesh.shape["win"]),
        mesh=mesh,
        in_specs=(P(None, "win", None, "grp"), P(), P(), P()),
        out_specs=P("win", None, "grp"),
        check_vma=False,
    )
```

```python
import functools
import math

import jax
import jax.numpy as jnp
import numpy as np
from jax import lax
from jax.experimental import pallas as pl
from jax.experimental.pallas import tpu as pltpu
from jax.sharding import PartitionSpec as P

MESH = pl.DeviceIdType.MESH
GY = 64
N_X = 4
LANES = 128
SHOTS = 4
F32, BF16 = jnp.float32, jnp.bfloat16


def split(table):
    high = table.astype(BF16)
    return high, (table - high.astype(F32)).astype(BF16)


def dot(a, b):
    return jnp.dot(a, b, preferred_element_type=F32)


def dot_lanes(a, b):
    return lax.dot_general(a, b, (((1,), (1,)), ((), ())), preferred_element_type=F32)


def dot3(a, b_high, b_low):
    high, low = split(a)
    width = b_high.shape[1]
    both = dot(high, jnp.concatenate([b_high, b_low], axis=1))
    return both[:, :width] + both[:, width:] + dot(low, b_high)


CODE_TOP = 32767.0
EXTRA = 16


def coded(block):
    top = jnp.max(jnp.abs(block), axis=0, keepdims=True)
    exponent = jnp.ceil(jnp.log2(jnp.maximum(top, 1e-30)))
    values = jnp.round(block * (CODE_TOP * jnp.exp2(-exponent)))
    return jnp.concatenate([values, jnp.broadcast_to(exponent, (EXTRA, LANES))], axis=0).astype(jnp.int32).astype(jnp.int16)


def decoded(code):
    values = code.astype(jnp.int32).astype(F32)
    rows = code.shape[0] - EXTRA
    return values[:rows] * (jnp.exp2(values[rows : rows + 1]) * (1.0 / CODE_TOP))


def np_split(table):
    table = table.astype(np.float32)
    high = table.astype(BF16)
    return high, (table - high.astype(np.float32)).astype(BF16)


def tables(grid_x):
    def angles(length):
        index = np.arange(length)
        return (index[:, None] * index[None, :] % length) * (2.0 * math.pi / length)

    cos_x, sin_x = np.cos(angles(grid_x)), np.sin(angles(grid_x))
    cos_y, sin_y = np.cos(angles(GY)), np.sin(angles(GY))
    shots = np.eye(SHOTS)
    block_cos, block_sin = np.kron(shots, cos_x), np.kron(shots, sin_x)
    rows_y = np.concatenate([cos_y, sin_y], axis=0)
    forward_x = np.concatenate([block_cos, block_sin], axis=1)
    inverse_x = np.concatenate([block_cos, -block_sin], axis=1)
    to_re = np.concatenate([cos_y, -sin_y], axis=0)
    to_im = np.concatenate([sin_y, cos_y], axis=0)
    none = np.zeros_like(to_re)
    inverse_y = np.block([[to_re, none, to_im, none], [none, to_re, none, to_im]])
    x_index, y_index = np.arange(grid_x), np.arange(GY)
    x_signed = np.where(x_index < (grid_x + 1) // 2, x_index, x_index - grid_x).astype(np.float32) * np.float32(
        2.0 * math.pi / grid_x
    )
    y_signed = np.where(y_index < (GY + 1) // 2, y_index, y_index - GY).astype(np.float32) * np.float32(
        2.0 * math.pi / GY
    )
    squares = x_signed[:, None] ** 2 + y_signed[None, :] ** 2
    return (
        np.stack(np_split(rows_y)),
        np.stack(np_split(forward_x)),
        np.stack(np_split(inverse_x)),
        np.stack(np_split(inverse_y)),
        np.concatenate([squares, squares], axis=1).astype(np.float32),
    )


def iota(shape, dim):
    return lax.broadcasted_iota(jnp.int32, shape, dim)


def one_hot(condition):
    return jnp.where(condition, 1.0, 0.0).astype(BF16)


def kernel(
    n_grp, n_win, windows,
    spectra, positions_hbm, freq_hbm, slowness_hbm, rows_hbm, forward_hbm, inverse_x_hbm, inverse_y_hbm, squares_hbm,
    out,
    positions, freq_bins, slowness, rows_y, forward_x, inverse_x, inverse_y, squares,
    u, v, picked, theirs, own_gram, blocks, got_blocks, tiles, got_tiles, energy, got_energy,
    y_phase, x_mask, shift,
    local_sem, core_sem, pick_send, pick_recv, first_send, first_recv, second_send, second_recv, rs_send, rs_recv, tile_sem, energy_sem,
):
    n_freq = n_win // 2
    n_y = n_freq // 2
    n_z = n_grp // N_X
    n_src = SHOTS * n_grp
    grid_x = 2 * n_grp
    receivers = n_grp * LANES
    rows = 2 * windows
    win, grp = lax.axis_index("win"), lax.axis_index("grp")
    core, chip = lax.rem(win, 2), lax.div(win, 2)
    z_low, y = lax.rem(chip, 2), lax.div(chip, 2)
    zh, x = lax.rem(grp, n_z), lax.div(grp, n_z)
    other = 1 - core

    def at_y(d):
        return lax.rem(y + d + n_y, n_y)

    def at_x(d):
        return lax.rem(x + d + N_X, N_X)

    def at_zh(d):
        return lax.rem(zh + d + n_z, n_z)

    def device(chip_at, core_at, grp_at):
        return (chip_at * 2 + core_at, grp_at)

    def remote(src, dst, send_sem, recv_sem, target):
        return pltpu.make_async_remote_copy(
            src_ref=src, dst_ref=dst, send_sem=send_sem, recv_sem=recv_sem, device_id=target, device_id_type=MESH
        )

    ends = []

    def send(copy):
        copy.start()
        ends.append(copy)

    def send_all(copies, whole):
        for copy in copies:
            copy.start()
        ends.append(whole)

    def drain():
        for copy in ends:
            copy.wait_send()
        ends.clear()

    def hops(offset):
        return min(offset[0], N_X - offset[0]) + 2 * min(offset[1], n_z - offset[1])

    offsets = sorted(((a, b) for a in range(N_X) for b in range(n_z)), key=hops, reverse=True)
    away = offsets[:-1]
    far_z = sorted(range(1, n_z), key=lambda d: -min(d, n_z - d))
    far_x = sorted(range(1, N_X), key=lambda d: -min(d, N_X - d))

    def to(offset):
        return at_x(offset[0]) * n_z + at_zh(offset[1])

    partner = device(chip, other, grp)
    loads = [
        pltpu.make_async_copy(source, target, local_sem.at[i])
        for i, (source, target) in enumerate(
            (
                (spectra.at[:, core], u.at[:, core]),
                (spectra.at[:, other], v),
                (positions_hbm, positions),
                (freq_hbm, freq_bins),
                (slowness_hbm, slowness),
                (rows_hbm, rows_y),
                (forward_hbm, forward_x),
                (inverse_x_hbm, inverse_x),
                (inverse_y_hbm, inverse_y),
                (squares_hbm, squares),
            )
        )
    ]
    for load in loads:
        load.start()

    barrier = pltpu.get_barrier_semaphore()
    greeted = [device(chip, core, to(o)) for o in away]
    greeted += [device(y * 2 + 1 - z_low, core, to(o)) for o in away]
    greeted += [device(at_y(d) * 2 + z_low, core, grp) for d in (2, -2, 1, -1)]
    greeted += [device(y * 2 + 1 - z_low, core, grp), partner]
    greeted += [device(chip, other, to(o)) for o in away if 0 in o]
    for target in greeted:
        pl.semaphore_signal(barrier, inc=1, device_id=target, device_id_type=MESH)

    ahead = [4, 3, -3, 2, 1, -2, -1, 0]
    assert n_y == len(ahead)
    slots = [(d, z) for d in ahead for z in range(2)]
    chunk = 16 // SHOTS
    n_chunk = n_freq // chunk

    def freq_of(slot):
        return at_y(slots[slot][0]) * 2 + slots[slot][1]

    loads[0].wait()
    loads[1].wait()
    row, lane = iota((n_freq * SHOTS, LANES), 0), iota((n_freq * SHOTS, LANES), 1)
    own = jnp.zeros((n_freq * SHOTS, rows), F32)
    for_partner = jnp.zeros((n_freq * SHOTS, rows), F32)
    for slot in range(n_freq):
        pick = one_hot(lane == (row - SHOTS * slot) * (LANES // SHOTS))
        own += dot_lanes(pick, u[freq_of(slot), core])
        for_partner += dot_lanes(pick, v[freq_of(slot)])
    own, for_partner = own.astype(BF16), for_partner.astype(BF16)
    for c in range(n_chunk):
        picked[c, x, 0, core] = own[16 * c : 16 * c + 16]
        theirs[c] = for_partner[16 * c : 16 * c + 16]

    pl.semaphore_wait(barrier, len(greeted))

    mixed = n_chunk - 1

    def first_copy(c, axis, d, to_core):
        peer = to((d, 0) if axis == 0 else (0, d))
        source = picked.at[c, x, 0, core] if to_core == 0 else theirs.at[c]
        return remote(
            source, picked.at[c, x, (n_z - d) % n_z if axis else 0, core], first_send.at[c, axis], first_recv.at[c, axis],
            device(chip, other if to_core else core, peer),
        )

    def first_whole(c, axis):
        part = picked.at[c, x, 1:] if axis else picked.at[c, 1:, 0]
        return remote(part, part, first_send.at[c, axis], first_recv.at[c, axis], partner)

    def first_start(c, axis):
        send_all(
            [first_copy(c, axis, d, to_core) for d in (far_z if axis else far_x) for to_core in range(2)],
            first_whole(c, axis),
        )

    def second_copy(c, d):
        if c == mixed:
            source, target, offset = picked.at[c, :, 0], picked.at[c, :, n_z - d], (0, d)
        else:
            source, target, offset = picked.at[c, x, 1:], picked.at[c, x, 1:], (d, 0)
        return remote(source, target, second_send.at[c], second_recv.at[c], device(chip, core, to(offset)))

    def second_whole(c):
        part = picked.at[c, :, 1:] if c == mixed else picked.at[c, 1:, 1:]
        return remote(part, part, second_send.at[c], second_recv.at[c], partner)

    def second_start(c):
        send_all([second_copy(c, d) for d in (far_z if c == mixed else far_x)], second_whole(c))

    def second_wait(c):
        second_whole(c).wait_recv()
        if c != mixed:
            first_whole(c, 0).wait_recv()

    pick_copies = [
        remote(theirs.at[c], picked.at[c, x, 0, core], pick_send.at[c], pick_recv.at[c], partner) for c in range(n_chunk)
    ]
    core_copy = remote(v, u.at[:, core], core_sem.at[0], core_sem.at[1], partner)
    early = [0, mixed] + [c for c in range(1, n_chunk) if c != mixed]
    for c in early:
        send(pick_copies[c])
        first_start(c, 0 if c == mixed else 1)
    for c in range(n_chunk):
        if c != mixed:
            first_start(c, 0)
    send(core_copy)

    def side_tables():
        for load in loads[2:]:
            load.wait()
        where = positions[...]
        cell_x, cell_y = lax.shift_right_logical(where, 6), jnp.bitwise_and(where, GY - 1)
        y_hot = one_hot(iota((GY, receivers), 0) == cell_y)
        y_phase[0:LANES] = dot(rows_y[0], y_hot).astype(BF16)
        y_phase[LANES:] = dot(rows_y[1], y_hot).astype(BF16)
        x_mask[...] = one_hot(iota((grid_x, receivers), 0) == cell_x)
        freq = freq_bins[win].astype(F32)
        sign = jnp.where(iota((grid_x, LANES), 1) < GY, -1.0, 1.0)
        total_re, total_im = None, None
        for k in range(4):
            kappa = freq * slowness[k]
            excess = kappa * kappa - squares[...]
            vertical = jnp.sqrt(jnp.maximum(excess, 0.0))
            damping = jnp.exp(-jnp.sqrt(jnp.maximum(-excess, 0.0)))
            step_re, step_im = damping * jnp.cos(vertical), damping * jnp.sin(vertical)
            if k == 0:
                total_re, total_im = step_re, step_im
            else:
                total_re, total_im = total_re * step_re - total_im * step_im, total_re * step_im + total_im * step_re
            shift[k, 0] = total_re
            shift[k, 1] = sign * total_im

    height = 16 * n_grp
    row, lane = iota((height, height), 0), iota((height, height), 1)
    slot_of, src_of = lax.div(row, n_src), lax.rem(row, n_src)
    origin = lax.div(src_of, SHOTS)
    held = lax.div(origin, n_z) * n_z + lax.rem(lax.rem(origin, n_z) + n_z - zh, n_z)
    reorder = one_hot(lane == held * 16 + slot_of * SHOTS + lax.rem(src_of, SHOTS))
    row, lane = iota((rows, rows), 0), iota((rows, rows), 1)
    even = lax.rem(row, 2) == 0
    turn = jnp.where(~even & (lane == row - 1), -1.0, jnp.where(even & (lane == row + 1), 1.0, 0.0)).astype(BF16)

    def grams(c):
        sources = []
        for half in range(2):
            plain = dot(reorder, picked[c, :, :, half].reshape(height, rows)).astype(BF16)
            sources.append((plain, dot(plain, turn).astype(BF16)))
        for i in range(chunk):
            slot = chunk * c + i
            q = freq_of(slot)
            result = None
            for half, (plain, turned) in enumerate(sources):
                left = jnp.concatenate([plain[n_src * i : n_src * (i + 1)], turned[n_src * i : n_src * (i + 1)]], axis=0)
                term = dot(left, u[q, half])
                result = term if result is None else result + term
            d, z = slots[slot]
            if abs(d) == 2:
                for passed in ((2 * d, 3 * d // 2) if (d > 0) == (z == 0) else (3 * d // 2,)):
                    result += block_arrived(slots.index((abs(passed) if passed == -4 else passed, z)))
            if d:
                block_send(slot, result)
            else:
                own_gram[z] = result

    def block_copy(slot):
        d, z = slots[slot]
        step = ((2 if z == 0 else -2) if d == 4 else d // 3) if abs(d) > 2 else d
        target, index = at_y(step) * 2 + z_low, slot
        return remote(
            blocks.at[slot], got_blocks.at[index], rs_send.at[slot], rs_recv.at[index], device(target, core, grp)
        )

    def block_send(slot, value):
        blocks[slot] = coded(value)
        send(block_copy(slot))

    def block_arrived(index):
        remote(
            blocks.at[0], got_blocks.at[index], rs_send.at[0], rs_recv.at[index], device(at_y(1) * 2 + z_low, core, grp)
        ).wait_recv()
        return decoded(got_blocks[index])

    for c in early:
        pick_copies[c].wait_recv()
        first_whole(c, 0 if c == mixed else 1).wait_recv()
        second_start(c)
    side_tables()
    core_copy.wait_recv()
    for c in range(n_chunk):
        second_wait(c)
        grams(c)
    totals = []
    for z in range(2):
        total = own_gram[z]
        for d in (2, 1, -2, -1):
            total += block_arrived(slots.index((d, z)))
        totals.append(total)

    here = z_low == 0
    upper = lax.rem(iota((n_src, LANES), 0), 8) < SHOTS
    for kind, total in enumerate((jnp.where(here, totals[0], totals[1]), jnp.where(here, totals[1], totals[0]))):
        real, imag = total[:n_src], total[n_src:]
        first = jnp.where(upper, real, pltpu.roll(imag, SHOTS, 0))
        second = jnp.where(upper, pltpu.roll(real, n_src - SHOTS, 0), imag)
        for a in range(n_grp // 2):
            tiles[kind * n_grp + 2 * a] = first[8 * a : 8 * a + 8]
            tiles[kind * n_grp + 2 * a + 1] = second[8 * a : 8 * a + 8]

    def tile_copy(kind, offset):
        target = to(offset)
        z = z_low if kind == 0 else 1 - z_low
        return remote(
            tiles.at[kind * n_grp + target], got_tiles.at[kind * n_grp + grp], tile_sem.at[0], tile_sem.at[1],
            device(y * 2 + z, core, target),
        )

    tiles_whole = remote(tiles.at[1:], got_tiles.at[1:], tile_sem.at[0], tile_sem.at[1], partner)
    got_tiles[grp] = tiles[grp]
    before = list(ends)
    ends.clear()
    send_all([tile_copy(kind, o) for o in offsets for kind in (0, 1) if kind or o != (0, 0)], tiles_whole)
    for copy in before:
        copy.wait_send()
    tiles_whole.wait_recv()

    field = jnp.concatenate([got_tiles[g] + got_tiles[n_grp + g] for g in range(n_grp)], axis=1)
    field_high = field.astype(BF16).astype(F32)
    field_low = field - field_high
    mask = x_mask[...]

    def placed(part):
        return jnp.concatenate(
            [jnp.broadcast_to(part[i : i + 1], (grid_x, receivers)).astype(BF16) * mask for i in range(2 * SHOTS)], axis=0
        )

    section = dot_lanes(placed(field_high), y_phase[...])
    section = section[:, :LANES] + section[:, LANES:] + dot_lanes(placed(field_low), y_phase[0:LANES])
    half = SHOTS * grid_x
    lower = iota((half, LANES), 1) < GY
    plus_minus = jnp.where(lower, 1.0, -1.0)
    section = plus_minus * section[:half] + pltpu.roll(section[half:], GY, 1)
    turned_section = plus_minus * pltpu.roll(section, GY, 1)
    stacked = jnp.concatenate([section, turned_section], axis=0)
    stacked_high, stacked_low = split(stacked)
    both = dot(forward_x[0], jnp.concatenate([stacked_high, stacked_low], axis=1))
    spec = both[:, :LANES] + both[:, LANES:] + dot(forward_x[1], stacked_high)
    spec_turned = pltpu.roll(spec, GY, 1)
    spec3, spec3_turned = spec.reshape(SHOTS, grid_x, LANES), spec_turned.reshape(SHOTS, grid_x, LANES)
    for p in range(2):
        shifted = [
            (spec3 * shift[k, 0][None] + spec3_turned * shift[k, 1][None]).reshape(half, LANES) for k in (2 * p, 2 * p + 1)
        ]
        back = dot3(jnp.concatenate(shifted, axis=1), inverse_y[0], inverse_y[1])
        back = jnp.concatenate([back[:, :LANES], back[:, LANES:]], axis=0)
        back_high, back_low = split(back)
        both = dot(inverse_x[0], jnp.concatenate([back_high, back_low], axis=1))
        picture = both[:, :LANES] + both[:, LANES:] + dot(inverse_x[1], back_high)
        energies = jnp.sum((picture * picture).reshape(SHOTS, grid_x, LANES), axis=0)
        for g in range(n_grp):
            energy[g, 2 * p : 2 * p + 2] = energies[2 * g : 2 * g + 2]

    def energy_copy(i):
        target = to(away[i])
        return remote(
            energy.at[target], got_energy.at[i], energy_sem.at[0], energy_sem.at[1], device(chip, core, target)
        )

    energy_whole = remote(energy.at[1:], got_energy.at[: n_grp - 1], energy_sem.at[0], energy_sem.at[1], partner)
    send_all([energy_copy(i) for i in range(n_grp - 1)], energy_whole)
    image = energy[grp]
    energy_whole.wait_recv()
    for i in range(n_grp - 1):
        image += got_energy[i]
    n_windows = windows * n_win
    scale = 1.0 / (n_src * grid_x * GY * n_windows * n_windows)
    for p in range(2):
        one, two = image[2 * p : 2 * p + 1] * scale, image[2 * p + 1 : 2 * p + 2] * scale
        low = iota((1, LANES), 1) < GY
        out[2 * p : 2 * p + 1] = jnp.where(low, one, pltpu.roll(two, GY, 1))
        out[2 * p + 1 : 2 * p + 2] = jnp.where(low, pltpu.roll(one, GY, 1), two)

    drain()


def body(n_grp, n_win, spectra, freq_bins, slowness, positions):
    freqs, windows, _, block = spectra.shape
    grid_x = 2 * n_grp
    n_freq = n_win // 2
    n_chunk = n_freq * SHOTS // 16
    n_z = n_grp // N_X
    rows = 2 * windows
    n_src = SHOTS * n_grp
    receivers = n_grp * block
    hbm = pl.BlockSpec(memory_space=pltpu.HBM)
    dma = pltpu.SemaphoreType.DMA
    consts = tables(grid_x)
    image = pl.pallas_call(
        functools.partial(kernel, n_grp, n_win, windows),
        out_shape=jax.ShapeDtypeStruct((4, block), F32),
        in_specs=[hbm] * (4 + len(consts)),
        out_specs=pl.BlockSpec(memory_space=pltpu.VMEM),
        scratch_shapes=[
            pltpu.VMEM((1, receivers), jnp.int32),
            pltpu.SMEM((n_win,), jnp.int32),
            pltpu.SMEM((4,), F32),
            *(pltpu.VMEM(c.shape, c.dtype) for c in consts),
            pltpu.VMEM((n_freq, 2, rows, block), BF16),
            pltpu.VMEM((n_freq, rows, block), BF16),
            pltpu.VMEM((n_chunk, N_X, n_z, 2, 16, rows), BF16),
            pltpu.VMEM((n_chunk, 16, rows), BF16),
            pltpu.VMEM((2, 2 * n_src, block), F32),
            pltpu.VMEM((n_freq, 2 * n_src + EXTRA, block), jnp.int16),
            pltpu.VMEM((n_freq, 2 * n_src + EXTRA, block), jnp.int16),
            pltpu.VMEM((2 * n_grp, 2 * SHOTS, block), F32),
            pltpu.VMEM((2 * n_grp, 2 * SHOTS, block), F32),
            pltpu.VMEM((n_grp, SHOTS, block), F32),
            pltpu.VMEM((n_grp, SHOTS, block), F32),
            pltpu.VMEM((2 * LANES, receivers), BF16),
            pltpu.VMEM((grid_x, receivers), BF16),
            pltpu.VMEM((4, 2, grid_x, LANES), F32),
            dma((5 + len(consts),)), dma((2,)), dma((n_chunk,)), dma((n_chunk,)),
            dma((n_chunk, 2)), dma((n_chunk, 2)), dma((n_chunk,)), dma((n_chunk,)),
            dma((n_freq,)), dma((n_freq,)),
            dma((2,)), dma((2,)),
        ],
        compiler_params=pltpu.CompilerParams(
            collective_id=0, has_side_effects=True, vmem_limit_bytes=63 * 1024 * 1024
        ),
    )(
        spectra.reshape(n_freq, 2, rows, block),
        positions.reshape(1, receivers),
        freq_bins,
        slowness,
        *(jnp.asarray(c) for c in consts),
    )
    return image[None]


def solution(mesh):
    return jax.shard_map(
        functools.partial(body, mesh.shape["grp"], mesh.shape["win"]),
        mesh=mesh,
        in_specs=(P(None, "win", None, "grp"), P(), P(), P()),
        out_specs=P("win", None, "grp"),
        check_vma=False,
    )
```
